32 devices in a mesh: rep: 8 (over z, x), fsdp: 4 (over y, core).
Axes of the slice: x: 2, y: 2, z: 4, core: 2. Of those that a mesh axis runs over, the one named last changes fastest.
Arguments:
- activations: bfloat16 [8, 768, 4096], P('rep', 'fsdp'), may hold values from -6 to 6
- weights: float32 [8, 4096, 512], P('rep', 'fsdp'), may hold values from -6 to 6
- cotangent: bfloat16 [8, 768, 512], P('rep', 'fsdp'), may hold values from -6 to 6
- step_index: int32 [1], replicated, may hold values from 0 to 999
Outputs:
- projected: bfloat16 [8, 768, 512], P('rep', 'fsdp')
- input_grad: bfloat16 [8, 768, 4096], P('rep', 'fsdp')
- mixed: float32 [8, 4096, 512], P('rep', 'fsdp')
The draws below stay inside these ranges and needn't reach their ends.
All inputs are finite; a program needn't handle non-finite values.
Results may differ from the reference program's by a relative error of at most 0.005.
Values may be sent and summed in bfloat16 or wider, within the bound.
A program may use at most 64 MiB of HBM per device.

```python
import jax
import jax.numpy as jnp
from jax import lax

D = 4096
KW = 512
TOK_DEV = 192
TOKENS = 768
REPLICAS = 8
BITS = 3
N_FSDP = 4


def spiked(drawn, key, source, target, parts, factor):
    def block_of(position):
        return (jnp.arange(drawn.shape[position]) // (drawn.shape[position] // parts)).reshape((-1,) + (1,) * (drawn.ndim - 1 - position))

    near = jax.random.permutation(key, parts)[block_of(target)]
    far = (block_of(target) + parts // 2) % parts
    return jnp.where((block_of(source) == near) | (block_of(source) == far), factor * drawn, drawn)


def shard_levels(rng, dims, split, low, high):
    level, own = 1.0, jax.random.fold_in(rng, 6)
    for axis_at, blocks in split:
        steps = jnp.exp(jax.random.uniform(jax.random.fold_in(own, axis_at), (blocks,), jnp.float32, low / len(split), high / len(split)))
        level = level * jnp.repeat(steps, dims[axis_at] // blocks).reshape([-1 if axis == axis_at else 1 for axis in range(len(dims))])
    return level


def centred(rng, dims, width, most, shards=(), kind=jnp.bfloat16):
    array = jax.random.normal(rng, dims, jnp.float32) * width
    if len(shards) > 0:
        array = shard_levels(rng, dims, shards, -0.22, 0.18) * array
    return jnp.clip(array, min=-most, max=most).astype(kind)


def noise_with(key, shape, scale, limit, pieces, heavy, held_as=jnp.bfloat16):
    array = scale * jax.random.normal(key, shape, jnp.float32)
    if pieces:
        array = array * shard_levels(key, shape, pieces, -0.22, 0.18)
    return jnp.clip(spiked(array, jax.random.fold_in(key, 3), *heavy), -limit, limit).astype(held_as)


def setup_inputs(seed: int = 0) -> dict:
    splits = jax.random.split(jax.random.key(seed), 5)
    return {
        "activations": noise_with(splits[0], (REPLICAS, TOKENS, D), 1.0, 6.0, ((0, 8), (1, 4)), (1, 2, 4, 2.0)),
        "weights": centred(splits[1], (REPLICAS, D, KW), 1.0, 6.0, ((0, 8), (1, 4)), jnp.float32),
        "cotangent": centred(splits[2], (REPLICAS, TOKENS, KW), 1.0, 6.0, ((0, 8), (1, 4))),
        "step_index": jax.random.randint(splits[3], (1,), 0, 1000).astype(jnp.int32),
    }


def one_replica(items):
    inputs, master, cotan, rate = items
    scale = D ** (-0.5)
    half_weights = master.astype(jnp.bfloat16)
    projected = (jnp.dot(inputs, half_weights, preferred_element_type=jnp.float32) * scale).astype(jnp.bfloat16)
    back = jnp.dot(cotan, half_weights.T, preferred_element_type=jnp.float32)
    input_grad = (back * scale).astype(jnp.bfloat16)
    blocks_in = inputs.reshape(N_FSDP, TOK_DEV, D).astype(jnp.float32)
    blocks_co = cotan.reshape(N_FSDP, TOK_DEV, KW).astype(jnp.float32)
    partial_terms = (jnp.einsum('btd,btk->bdk', blocks_in, blocks_co) * scale).astype(jnp.bfloat16)
    partial_terms = lax.optimization_barrier(partial_terms)
    grad = lax.optimization_barrier(jnp.sum(partial_terms.astype(jnp.float32), axis=0))
    updated = master - rate * grad
    return (projected, input_grad, updated)

def reference(activations, weights, cotangent, step_index):
    rate = 0.3 / jnp.sqrt(1.0 + step_index[0].astype(jnp.float32) / 50.0)
    rates = jnp.full((REPLICAS,), rate, dtype=jnp.float32)
    projected, input_grad, updated = lax.map(one_replica, (activations, weights, cotangent, rates))
    bit = step_index[0] % BITS
    partners = jnp.arange(REPLICAS, dtype=jnp.int32) ^ jnp.left_shift(jnp.int32(1), bit)
    mixed = 0.5 * (updated + jnp.take(updated, partners, axis=0))
    return (projected, input_grad, mixed)
```

```python
import functools

import jax
import jax.numpy as jnp
from jax import lax
from jax.experimental import pallas as pl
from jax.experimental.pallas import tpu as pltpu
from jax.sharding import PartitionSpec as P

BITS = 3
MESH = pl.DeviceIdType.MESH
BF16 = jnp.bfloat16
F32 = jnp.float32


def kernel(
    bit, chips, chunks, scale,
    step_ref, act_hbm, w_hbm, cot_hbm,
    proj_ref, ig_hbm, mixed_hbm,
    act, cot, w, wb, ig, part, to_sib, from_sib, to_chip, from_chip, upd, give, take,
    local_sem, cot_send, cot_recv, act_send, act_recv, ig_send, ig_recv,
    sib_send, sib_recv, chip_send, chip_recv, give_sem, take_sem, out_sem,
):
    rep, me = lax.axis_index("rep"), lax.axis_index("fsdp")
    chip, core = me // 2, me % 2
    tokens = cot_hbm.shape[1]
    rows = w_hbm.shape[1]
    size = rows // chunks
    slots = 2 * chips
    half = 2 ** bit
    partner = rep + half - 2 * half * ((rep // half) % 2)

    def device(ahead, other):
        return ((chip + ahead + chips) % chips) * 2 + (core + other) % 2

    def sender(slot):
        return device(-(slot // 2), slot % 2)

    def receiver(slot):
        return device(slot // 2, slot % 2)

    def to_peer(src, dst, send, recv, peer):
        return pltpu.make_async_remote_copy(
            src_ref=src, dst_ref=dst, send_sem=send, recv_sem=recv,
            device_id=(rep, peer), device_id_type=MESH,
        )

    def of(slot):
        return pl.ds(slot * tokens, tokens)

    def cols(owner):
        return pl.ds(pl.multiple_of(owner * rows, rows), rows)

    def piece(owner, c):
        return pl.ds(pl.multiple_of(owner * rows + c * size, size), size)

    load_cot = pltpu.make_async_copy(cot_hbm.at[0], cot.at[of(0)], local_sem.at[0])
    load_act = pltpu.make_async_copy(act_hbm.at[0, :, cols(me)], act.at[of(0)], local_sem.at[1])
    load_w = pltpu.make_async_copy(w_hbm.at[0], w, local_sem.at[2])
    load_cot.start()
    load_w.start()
    load_act.start()

    barrier = pltpu.get_barrier_semaphore()
    for slot in range(1, slots):
        pl.semaphore_signal(barrier, inc=1, device_id=(rep, receiver(slot)), device_id_type=MESH)
    pl.semaphore_signal(barrier, inc=1, device_id=(partner, me), device_id_type=MESH)
    pl.semaphore_wait(barrier, slots)

    far = [slot for slot in range(2, slots)]
    order = far + [1]

    cot_copies = {}
    for ahead in range(1, chips):
        cot_copies[2 * ahead] = to_peer(
            cot_hbm.at[0], cot.at[of(2 * ahead)], cot_send.at[2 * ahead], cot_recv.at[2 * ahead], receiver(2 * ahead))
    cot_copies[1] = to_peer(cot_hbm.at[0], cot.at[of(1)], cot_send.at[1], cot_recv.at[1], receiver(1))
    for copy in cot_copies.values():
        copy.start()

    act_copies = {}

    def send_act(c):
        for slot in order:
            copy = to_peer(
                act_hbm.at[0, :, piece(receiver(slot), c)],
                act.at[of(slot), pl.ds(c * size, size)],
                act_send.at[c * slots + slot], act_recv.at[c * slots + slot], receiver(slot))
            copy.start()
            act_copies[c, slot] = copy

    send_act(0)
    if chunks > 1:
        send_act(1)

    load_w.wait()
    wb[...] = w[...].astype(BF16)
    load_cot.wait()
    load_act.wait()

    step = jnp.full((1, w.shape[1]), step_ref[0], jnp.int32).astype(F32)
    rate = 0.3 / jnp.sqrt(1.0 + step / 50.0)

    def input_grad(slot):
        ig[of(slot), :] = (lax.dot_general(
            cot[of(slot), :], wb[...], (((1,), (1,)), ((), ())), preferred_element_type=F32
        ) * scale).astype(BF16)

    input_grad(0)
    keep_ig = pltpu.make_async_copy(ig.at[of(0)], ig_hbm.at[0, :, cols(me)], out_sem.at[chunks])
    keep_ig.start()

    for ahead in range(1, chips):
        slot = 2 * ahead
        cot_copies[slot].wait_recv()
        forward = to_peer(
            cot.at[of(slot)], cot.at[of(slot + 1)], cot_send.at[slot + 1], cot_recv.at[slot + 1], device(0, 1))
        forward.start()
        cot_copies[slot + 1] = forward
        input_grad(slot)
    for slot in [1] + [2 * ahead + 1 for ahead in range(1, chips)]:
        cot_copies[slot].wait_recv()
        input_grad(slot)

    ig_copies = {}

    def send_ig(slot):
        copy = to_peer(
            ig.at[of(slot)], ig_hbm.at[0, :, cols(me)], ig_send.at[slot], ig_recv.at[slot], sender(slot))
        copy.start()
        ig_copies[slot] = copy

    send_ig(1)

    gossip = []
    for c in range(chunks):
        for slot in order:
            act_copies[c, slot].wait_recv()
        if c + 2 < chunks:
            send_act(c + 2)
        if c + 2 == max(chunks, 2):
            for slot in far:
                send_ig(slot)
        here = pl.ds(c * size, size)
        grad = lax.dot_general(
            act[:, here], cot[...], (((0,), (0,)), ((), ())), preferred_element_type=F32)
        new = w[here, :] - rate * (grad * scale)
        upd[here, :] = new
        give[here, :] = new.astype(BF16)
        copy = pltpu.make_async_remote_copy(
            src_ref=give.at[here], dst_ref=take.at[here], send_sem=give_sem.at[c], recv_sem=take_sem.at[c],
            device_id=(partner, me), device_id_type=MESH,
        )
        copy.start()
        gossip.append(copy)
        for slot in range(slots):
            term = lax.dot_general(
                act[of(slot), here], wb[here, :], (((1,), (0,)), ((), ())), preferred_element_type=F32)
            part[of(slot), :] = term if c == 0 else part[of(slot), :] + term

    if chunks == 1:
        for slot in far:
            if slot not in ig_copies:
                send_ig(slot)

    sib_copies = []
    for ahead in list(range(1, chips)) + [0]:
        here = pl.ds(ahead * tokens, tokens)
        to_sib[here, :] = part[of(2 * ahead + 1), :].astype(BF16)
        copy = to_peer(
            to_sib.at[here], from_sib.at[here], sib_send.at[ahead], sib_recv.at[ahead], device(0, 1))
        copy.start()
        sib_copies.append((ahead, copy))
    chip_copies = []
    for ahead, copy in sib_copies:
        here = pl.ds(ahead * tokens, tokens)
        copy.wait_recv()
        if ahead > 0:
            to_chip[here, :] = (part[of(2 * ahead), :] + from_sib[here, :].astype(F32)).astype(BF16)
            on = to_peer(
                to_chip.at[here], from_chip.at[here], chip_send.at[ahead], chip_recv.at[ahead], sender(2 * ahead))
            on.start()
            chip_copies.append((ahead, on))

    outs = [keep_ig]
    for c, copy in enumerate(gossip):
        here = pl.ds(c * size, size)
        copy.wait_recv()
        upd[here, :] = 0.5 * (upd[here, :] + take[here, :].astype(F32))
        out = pltpu.make_async_copy(upd.at[here], mixed_hbm.at[0, here], out_sem.at[c])
        out.start()
        outs.append(out)

    total = part[of(0), :] + from_sib[pl.ds(0, tokens), :].astype(F32)
    for ahead, on in chip_copies:
        on.wait_recv()
        total = total + from_chip[pl.ds(ahead * tokens, tokens), :].astype(F32)
    proj_ref[0] = (total * scale).astype(BF16)

    for copy in ig_copies.values():
        copy.wait_recv()
    for copy in outs:
        copy.wait()
    for copy in list(cot_copies.values()) + list(act_copies.values()) + list(ig_copies.values()):
        copy.wait_send()
    for copy in [copy for _, copy in sib_copies + chip_copies] + gossip:
        copy.wait_send()


def step_kernel(bit, count, activations, weights, cotangent, step_index):
    tokens, features = activations.shape[1:]
    rows, width = weights.shape[1:]
    chips = count // 2
    chunks = max(1, min(4, rows // 256))
    every = count * tokens
    dma = pltpu.SemaphoreType.DMA
    anywhere = pl.BlockSpec(memory_space=pl.ANY)
    return pl.pallas_call(
        functools.partial(kernel, bit, chips, chunks, features ** (-0.5)),
        out_shape=(
            jax.ShapeDtypeStruct((1, tokens, width), BF16),
            jax.ShapeDtypeStruct((1, tokens, features), BF16),
            jax.ShapeDtypeStruct((1, rows, width), F32),
        ),
        in_specs=[pl.BlockSpec(memory_space=pltpu.SMEM), anywhere, anywhere, anywhere],
        out_specs=(pl.BlockSpec(memory_space=pltpu.VMEM), anywhere, anywhere),
        scratch_shapes=[
            pltpu.VMEM((every, rows), BF16),
            pltpu.VMEM((every, width), BF16),
            pltpu.VMEM((rows, width), F32),
            pltpu.VMEM((rows, width), BF16),
            pltpu.VMEM((every, rows), BF16),
            pltpu.VMEM((every, width), F32),
            pltpu.VMEM((chips * tokens, width), BF16),
            pltpu.VMEM((chips * tokens, width), BF16),
            pltpu.VMEM((chips * tokens, width), BF16),
            pltpu.VMEM((chips * tokens, width), BF16),
            pltpu.VMEM((rows, width), F32),
            pltpu.VMEM((rows, width), BF16),
            pltpu.VMEM((rows, width), BF16),
            dma((3,)),
            dma((count,)), dma((count,)),
            dma((chunks * count,)), dma((chunks * count,)),
            dma((count,)), dma((count,)),
            dma((chips,)), dma((chips,)),
            dma((chips,)), dma((chips,)),
            dma((chunks,)), dma((chunks,)),
            dma((chunks + 1,)),
        ],
        compiler_params=pltpu.CompilerParams(
            collective_id=bit, has_side_effects=True, vmem_limit_bytes=48 * 2 ** 20),
        cost_estimate=pl.CostEstimate(
            flops=6 * every * rows * width, bytes_accessed=8 * 2 ** 20, transcendentals=0),
        name="step_bit_%d" % bit,
    )(step_index, activations, weights, cotangent)


def body(count, activations, weights, cotangent, step_index):
    branches = [functools.partial(step_kernel, bit, count) for bit in range(BITS)]
    return lax.switch(step_index[0] % BITS, branches, activations, weights, cotangent, step_index)


def solution(mesh):
    split = P("rep", "fsdp", None)
    return jax.shard_map(
        functools.partial(body, mesh.shape["fsdp"]),
        mesh=mesh,
        in_specs=(split, split, split, P()),
        out_specs=(split, split, split),
        check_vma=False,
    )
```

```python
import functools

import jax
import jax.numpy as jnp
from jax import lax
from jax.experimental import pallas as pl
from jax.experimental.pallas import tpu as pltpu
from jax.sharding import PartitionSpec as P

BITS = 3
MESH = pl.DeviceIdType.MESH
BF16 = jnp.bfloat16
F32 = jnp.float32


def kernel(
    bit, chips, chunks, scale,
    step_ref, act_hbm, w_hbm, cot_hbm,
    proj_ref, ig_ref, mixed_ref,
    act, cot, w, wb, ig, part, to_sib, from_sib, to_chip, from_chip, give, take,
    local_sem, cot_send, cot_recv, act_send, act_recv, ig_send, ig_recv,
    sib_send, sib_recv, chip_send, chip_recv, give_sem, take_sem,
):
    rep, me = lax.axis_index("rep"), lax.axis_index("fsdp")
    chip, core = me // 2, me % 2
    tokens = cot_hbm.shape[1]
    rows = w_hbm.shape[1]
    size = rows // chunks
    slots = 2 * chips
    half = 2 ** bit
    partner = rep + half - 2 * half * ((rep // half) % 2)

    def device(ahead, other):
        return ((chip + ahead + chips) % chips) * 2 + (core + other) % 2

    def sender(slot):
        return device(-(slot // 2), slot % 2)

    def receiver(slot):
        return device(slot // 2, slot % 2)

    def to_peer(src, dst, send, recv, peer):
        return pltpu.make_async_remote_copy(
            src_ref=src, dst_ref=dst, send_sem=send, recv_sem=recv,
            device_id=(rep, peer), device_id_type=MESH,
        )

    def of(slot):
        return pl.ds(slot * tokens, tokens)

    def cols(owner):
        return pl.ds(pl.multiple_of(owner * rows, rows), rows)

    def piece(owner, c):
        return pl.ds(pl.multiple_of(owner * rows + c * size, size), size)

    load_cot = pltpu.make_async_copy(cot_hbm.at[0], cot.at[of(0)], local_sem.at[0])
    load_act = pltpu.make_async_copy(act_hbm.at[0, :, cols(me)], act.at[of(0)], local_sem.at[1])
    load_w = pltpu.make_async_copy(w_hbm.at[0], w, local_sem.at[2])
    load_cot.start()
    load_w.start()
    load_act.start()

    barrier = pltpu.get_barrier_semaphore()
    for slot in range(1, slots):
        pl.semaphore_signal(barrier, inc=1, device_id=(rep, receiver(slot)), device_id_type=MESH)
    pl.semaphore_signal(barrier, inc=1, device_id=(partner, me), device_id_type=MESH)
    pl.semaphore_wait(barrier, slots)

    far = [slot for slot in range(2, slots)]
    order = far + [1]

    cot_copies = {}
    for ahead in range(1, chips):
        cot_copies[2 * ahead] = to_peer(
            cot_hbm.at[0], cot.at[of(2 * ahead)], cot_send.at[2 * ahead], cot_recv.at[2 * ahead], receiver(2 * ahead))
    cot_copies[1] = to_peer(cot_hbm.at[0], cot.at[of(1)], cot_send.at[1], cot_recv.at[1], receiver(1))
    for copy in cot_copies.values():
        copy.start()

    act_copies = {}

    def send_act(c):
        for slot in order:
            copy = to_peer(
                act_hbm.at[0, :, piece(receiver(slot), c)],
                act.at[of(slot), pl.ds(c * size, size)],
                act_send.at[c * slots + slot], act_recv.at[c * slots + slot], receiver(slot))
            copy.start()
            act_copies[c, slot] = copy

    send_act(0)
    if chunks > 1:
        send_act(1)

    load_w.wait()
    wb[...] = w[...].astype(BF16)
    load_cot.wait()
    load_act.wait()

    step = jnp.full((1, w.shape[1]), step_ref[0], jnp.int32).astype(F32)
    rate = 0.3 / jnp.sqrt(1.0 + step / 50.0)

    def input_grad(slot):
        grad = (lax.dot_general(
            cot[of(slot), :], wb[...], (((1,), (1,)), ((), ())), preferred_element_type=F32
        ) * scale).astype(BF16)
        if slot == 0:
            ig_ref[0, :, cols(me)] = grad
        else:
            ig[of(slot - 1), :] = grad

    input_grad(0)

    for ahead in range(1, chips):
        slot = 2 * ahead
        cot_copies[slot].wait_recv()
        forward = to_peer(
            cot.at[of(slot)], cot.at[of(slot + 1)], cot_send.at[slot + 1], cot_recv.at[slot + 1], device(0, 1))
        forward.start()
        cot_copies[slot + 1] = forward
        input_grad(slot)
    for slot in [1] + [2 * ahead + 1 for ahead in range(1, chips)]:
        cot_copies[slot].wait_recv()
        input_grad(slot)

    ig_copies = {}

    def send_ig(slot):
        copy = to_peer(
            ig.at[of(slot - 1)], ig_ref.at[0, :, cols(me)], ig_send.at[slot], ig_recv.at[slot], sender(slot))
        copy.start()
        ig_copies[slot] = copy

    send_ig(1)

    gossip = []
    for c in range(chunks):
        for slot in order:
            act_copies[c, slot].wait_recv()
        if c + 2 < chunks:
            send_act(c + 2)
        if c + 2 == max(chunks, 2):
            for slot in far:
                send_ig(slot)
        here = pl.ds(c * size, size)
        grad = lax.dot_general(
            act[:, here], cot[...], (((0,), (0,)), ((), ())), preferred_element_type=F32)
        new = w[here, :] - rate * (grad * scale)
        mixed_ref[0, here, :] = new
        give[here, :] = new.astype(BF16)
        copy = pltpu.make_async_remote_copy(
            src_ref=give.at[here], dst_ref=take.at[here], send_sem=give_sem.at[c], recv_sem=take_sem.at[c],
            device_id=(partner, me), device_id_type=MESH,
        )
        copy.start()
        gossip.append(copy)
        for slot in range(slots):
            term = lax.dot_general(
                act[of(slot), here], wb[here, :], (((1,), (0,)), ((), ())), preferred_element_type=F32)
            part[of(slot), :] = term if c == 0 else part[of(slot), :] + term

    if chunks == 1:
        for slot in far:
            if slot not in ig_copies:
                send_ig(slot)

    sib_copies = []
    for ahead in list(range(1, chips)) + [0]:
        here = pl.ds(ahead * tokens, tokens)
        to_sib[here, :] = part[of(2 * ahead + 1), :].astype(BF16)
        copy = to_peer(
            to_sib.at[here], from_sib.at[here], sib_send.at[ahead], sib_recv.at[ahead], device(0, 1))
        copy.start()
        sib_copies.append((ahead, copy))
    chip_copies = []
    for ahead, copy in sib_copies:
        here = pl.ds(ahead * tokens, tokens)
        copy.wait_recv()
        if ahead > 0:
            to_chip[here, :] = (part[of(2 * ahead), :] + from_sib[here, :].astype(F32)).astype(BF16)
            on = to_peer(
                to_chip.at[here], from_chip.at[here], chip_send.at[ahead], chip_recv.at[ahead], sender(2 * ahead))
            on.start()
            chip_copies.append((ahead, on))

    for c, copy in enumerate(gossip):
        here = pl.ds(c * size, size)
        copy.wait_recv()
        mixed_ref[0, here, :] = 0.5 * (mixed_ref[0, here, :] + take[here, :].astype(F32))

    total = part[of(0), :] + from_sib[pl.ds(0, tokens), :].astype(F32)
    for ahead, on in chip_copies:
        on.wait_recv()
        total = total + from_chip[pl.ds(ahead * tokens, tokens), :].astype(F32)
    proj_ref[0] = (total * scale).astype(BF16)

    for copy in ig_copies.values():
        copy.wait_recv()
    for copy in list(cot_copies.values()) + list(act_copies.values()) + list(ig_copies.values()):
        copy.wait_send()
    for copy in [copy for _, copy in sib_copies + chip_copies] + gossip:
        copy.wait_send()


def store_kernel(proj_ref, ig_ref, mixed_ref, proj_hbm, ig_hbm, mixed_hbm, sem):
    copies = [pltpu.make_async_copy(proj_ref, proj_hbm, sem.at[0])]
    for src, dst in ((ig_ref, ig_hbm), (mixed_ref, mixed_hbm)):
        size = src.shape[1] // 4
        for c in range(4):
            here = pl.ds(c * size, size)
            copies.append(pltpu.make_async_copy(src.at[0, here], dst.at[0, here], sem.at[len(copies)]))
    for copy in copies:
        copy.start()
    for copy in copies:
        copy.wait()


def step_kernel(bit, count, activations, weights, cotangent, step_index):
    tokens, features = activations.shape[1:]
    rows, width = weights.shape[1:]
    chips = count // 2
    chunks = max(1, min(4, rows // 256))
    every = count * tokens
    dma = pltpu.SemaphoreType.DMA
    anywhere = pl.BlockSpec(memory_space=pl.ANY)
    in_vmem = pl.BlockSpec(memory_space=pltpu.VMEM)
    results = pl.pallas_call(
        functools.partial(kernel, bit, chips, chunks, features ** (-0.5)),
        out_shape=(
            pltpu.VMEM((1, tokens, width), BF16),
            pltpu.VMEM((1, tokens, features), BF16),
            pltpu.VMEM((1, rows, width), F32),
        ),
        in_specs=[pl.BlockSpec(memory_space=pltpu.SMEM), anywhere, anywhere, anywhere],
        out_specs=(in_vmem, in_vmem, in_vmem),
        scratch_shapes=[
            pltpu.VMEM((every, rows), BF16),
            pltpu.VMEM((every, width), BF16),
            pltpu.VMEM((rows, width), F32),
            pltpu.VMEM((rows, width), BF16),
            pltpu.VMEM((every - tokens, rows), BF16),
            pltpu.VMEM((every, width), F32),
            pltpu.VMEM((chips * tokens, width), BF16),
            pltpu.VMEM((chips * tokens, width), BF16),
            pltpu.VMEM((chips * tokens, width), BF16),
            pltpu.VMEM((chips * tokens, width), BF16),
            pltpu.VMEM((rows, width), BF16),
            pltpu.VMEM((rows, width), BF16),
            dma((3,)),
            dma((count,)), dma((count,)),
            dma((chunks * count,)), dma((chunks * count,)),
            dma((count,)), dma((count,)),
            dma((chips,)), dma((chips,)),
            dma((chips,)), dma((chips,)),
            dma((chunks,)), dma((chunks,)),
        ],
        compiler_params=pltpu.CompilerParams(
            collective_id=bit, has_side_effects=True, vmem_limit_bytes=40 * 2 ** 20),
        cost_estimate=pl.CostEstimate(
            flops=6 * every * rows * width, bytes_accessed=8 * 2 ** 20, transcendentals=0),
        name="step_bit_%d" % bit,
    )(step_index, activations, weights, cotangent)
    return pl.pallas_call(
        store_kernel,
        out_shape=tuple(jax.ShapeDtypeStruct(part.shape, part.dtype) for part in results),
        in_specs=[anywhere] * 3,
        out_specs=(anywhere, anywhere, anywhere),
        scratch_shapes=[dma((9,))],
        compiler_params=pltpu.CompilerParams(vmem_limit_bytes=2 ** 20),
        name="store",
    )(*results)


def body(count, activations, weights, cotangent, step_index):
    branches = [functools.partial(step_kernel, bit, count) for bit in range(BITS)]
    return lax.switch(step_index[0] % BITS, branches, activations, weights, cotangent, step_index)


def solution(mesh):
    split = P("rep", "fsdp", None)
    return jax.shard_map(
        functools.partial(body, mesh.shape["fsdp"]),
        mesh=mesh,
        in_specs=(split, split, split, P()),
        out_specs=(split, split, split),
        check_vma=False,
    )
```

```python
import functools

import jax
import jax.numpy as jnp
from jax import lax
from jax.experimental import pallas as pl
from jax.experimental.pallas import tpu as pltpu
from jax.sharding import PartitionSpec as P

BITS = 3
MESH = pl.DeviceIdType.MESH
BF16 = jnp.bfloat16
F32 = jnp.float32


def kernel(
    bit, chips, chunks, scale,
    step_ref, act_hbm, w_hbm, cot_hbm,
    proj_ref, ig_ref, mixed_ref,
    act, cot, w, wb, ig, part, to_sib, from_sib, to_chip, from_chip, give, take,
    local_sem, cot_send, cot_recv, act_send, act_recv, ig_send, ig_recv,
    sib_send, sib_recv, chip_send, chip_recv, give_sem, take_sem,
):
    rep, me = lax.axis_index("rep"), lax.axis_index("fsdp")
    chip, core = me // 2, me % 2
    tokens = cot_hbm.shape[1]
    rows = w_hbm.shape[1]
    slots = 2 * chips
    half = 2 ** bit
    partner = rep + half - 2 * half * ((rep // half) % 2)

    def device(ahead, other):
        return ((chip + ahead + chips) % chips) * 2 + (core + other) % 2

    def sender(slot):
        return device(-(slot // 2), slot % 2)

    def receiver(slot):
        return device(slot // 2, slot % 2)

    def to_peer(src, dst, send, recv, peer):
        return pltpu.make_async_remote_copy(
            src_ref=src, dst_ref=dst, send_sem=send, recv_sem=recv,
            device_id=(rep, peer), device_id_type=MESH,
        )

    def of(slot):
        return pl.ds(slot * tokens, tokens)

    def cols(owner):
        return pl.ds(pl.multiple_of(owner * rows, rows), rows)

    def piece(owner, c):
        start, size = chunks[c].start, chunks[c].size
        return pl.ds(pl.multiple_of(owner * rows + start, 128), size)

    load_cot = pltpu.make_async_copy(cot_hbm.at[0], cot.at[of(0)], local_sem.at[0])
    load_act = pltpu.make_async_copy(act_hbm.at[0, :, cols(me)], act.at[of(0)], local_sem.at[1])
    load_w = pltpu.make_async_copy(w_hbm.at[0], w, local_sem.at[2])
    load_cot.start()
    load_w.start()
    load_act.start()

    barrier = pltpu.get_barrier_semaphore()
    for slot in range(1, slots):
        pl.semaphore_signal(barrier, inc=1, device_id=(rep, receiver(slot)), device_id_type=MESH)
    pl.semaphore_signal(barrier, inc=1, device_id=(partner, me), device_id_type=MESH)
    pl.semaphore_wait(barrier, slots)

    far = list(range(2, slots))
    order = far + [1]
    width = w.shape[1]
    halves = [pl.ds(0, width // 2), pl.ds(width // 2, width // 2)]
    cot_copies, act_copies, ig_copies = {}, {}, {}

    def start_cot(h, src, slot, peer):
        copy = to_peer(
            src, cot.at[of(slot), halves[h]],
            cot_send.at[h * slots + slot], cot_recv.at[h * slots + slot], peer)
        copy.start()
        cot_copies[h, slot] = copy

    def send_cot(h):
        for slot in list(range(2, slots, 2)) + [1]:
            start_cot(h, cot_hbm.at[0, :, halves[h]], slot, receiver(slot))

    def take_cot(h):
        for slot in range(2, slots, 2):
            cot_copies[h, slot].wait_recv()
            start_cot(h, cot.at[of(slot), halves[h]], slot + 1, device(0, 1))

    def wait_cot(h):
        for slot in range(1, slots, 2):
            cot_copies[h, slot].wait_recv()

    def send_act(c):
        for slot in order:
            copy = to_peer(
                act_hbm.at[0, :, piece(receiver(slot), c)],
                act.at[of(slot), chunks[c]],
                act_send.at[c * slots + slot], act_recv.at[c * slots + slot], receiver(slot))
            copy.start()
            act_copies[c, slot] = copy

    def wait_act(c):
        for slot in order:
            act_copies[c, slot].wait_recv()

    def input_grad(slot):
        grad = (lax.dot_general(
            cot[of(slot), :], wb[...], (((1,), (1,)), ((), ())), preferred_element_type=F32
        ) * scale).astype(BF16)
        if slot == 0:
            ig_ref[0, :, cols(me)] = grad
        else:
            ig[of(slot - 1), :] = grad

    def send_ig(slot):
        copy = to_peer(
            ig.at[of(slot - 1)], ig_ref.at[0, :, cols(me)], ig_send.at[slot], ig_recv.at[slot], sender(slot))
        copy.start()
        ig_copies[slot] = copy

    later = [functools.partial(send_act, c) for c in range(1, len(chunks))]

    def send_next(most=1):
        for _ in range(most):
            if later:
                later.pop(0)()

    gossip = []

    def update(here, across):
        grad = lax.dot_general(
            act[:, here], cot[:, across], (((0,), (0,)), ((), ())), preferred_element_type=F32)
        new = w[here, across] - rate[:, across.start:across.start + across.size] * (grad * scale)
        mixed_ref[0, here, across] = new
        give[here, across] = new.astype(BF16)
        at = len(gossip)
        copy = pltpu.make_async_remote_copy(
            src_ref=give.at[here, across], dst_ref=take.at[here, across],
            send_sem=give_sem.at[at], recv_sem=take_sem.at[at],
            device_id=(partner, me), device_id_type=MESH,
        )
        copy.start()
        gossip.append((here, across, copy))

    def project(c):
        here = chunks[c]
        for slot in range(slots):
            term = lax.dot_general(
                act[of(slot), here], wb[here, :], (((1,), (0,)), ((), ())), preferred_element_type=F32)
            part[of(slot), :] = term if c == 0 else part[of(slot), :] + term

    send_cot(0)
    send_act(0)
    send_cot(1)

    step = jnp.full((1, width), step_ref[0], jnp.int32).astype(F32)
    rate = 0.3 / jnp.sqrt(1.0 + step / 50.0)
    load_w.wait()
    load_cot.wait()
    load_act.wait()

    take_cot(0)
    send_next()
    wait_cot(0)
    wait_act(0)
    send_next()
    update(chunks[0], halves[0])
    take_cot(1)
    send_next()
    wb[...] = w[...].astype(BF16)
    wait_cot(1)
    update(chunks[0], halves[1])

    for c in range(1, len(chunks)):
        wait_act(c)
        send_next()
        update(chunks[c], pl.ds(0, width))
        if c == 1:
            for slot in order + [0]:
                input_grad(slot)
            send_ig(1)
            later += [functools.partial(send_ig, slot) for slot in far]
            project(0)
        project(c)
    send_next(len(later))

    sib_copies = []
    for ahead in list(range(1, chips)) + [0]:
        here = pl.ds(ahead * tokens, tokens)
        to_sib[here, :] = part[of(2 * ahead + 1), :].astype(BF16)
        copy = to_peer(
            to_sib.at[here], from_sib.at[here], sib_send.at[ahead], sib_recv.at[ahead], device(0, 1))
        copy.start()
        sib_copies.append((ahead, copy))
    chip_copies = []
    for ahead, copy in sib_copies:
        here = pl.ds(ahead * tokens, tokens)
        copy.wait_recv()
        if ahead > 0:
            to_chip[here, :] = (part[of(2 * ahead), :] + from_sib[here, :].astype(F32)).astype(BF16)
            on = to_peer(
                to_chip.at[here], from_chip.at[here], chip_send.at[ahead], chip_recv.at[ahead], sender(2 * ahead))
            on.start()
            chip_copies.append((ahead, on))

    for here, across, copy in gossip:
        copy.wait_recv()
        mixed_ref[0, here, across] = 0.5 * (mixed_ref[0, here, across] + take[here, across].astype(F32))

    total = part[of(0), :] + from_sib[pl.ds(0, tokens), :].astype(F32)
    for ahead, on in chip_copies:
        on.wait_recv()
        total = total + from_chip[pl.ds(ahead * tokens, tokens), :].astype(F32)
    proj_ref[0] = (total * scale).astype(BF16)

    for copy in ig_copies.values():
        copy.wait_recv()
    for copy in list(cot_copies.values()) + list(act_copies.values()) + list(ig_copies.values()):
        copy.wait_send()
    for copy in [copy for _, copy in sib_copies + chip_copies] + [copy for _, _, copy in gossip]:
        copy.wait_send()


def store_kernel(proj_ref, ig_ref, mixed_ref, proj_hbm, ig_hbm, mixed_hbm, sem):
    copies = [pltpu.make_async_copy(proj_ref, proj_hbm, sem.at[0])]
    for src, dst in ((ig_ref, ig_hbm), (mixed_ref, mixed_hbm)):
        size = src.shape[1] // 4
        for c in range(4):
            here = pl.ds(c * size, size)
            copies.append(pltpu.make_async_copy(src.at[0, here], dst.at[0, here], sem.at[len(copies)]))
    for copy in copies:
        copy.start()
    for copy in copies:
        copy.wait()


def step_kernel(bit, count, activations, weights, cotangent, step_index):
    tokens, features = activations.shape[1:]
    rows, width = weights.shape[1:]
    chips = count // 2
    chunks = [pl.ds(start, 128) for start in range(0, min(rows, 256), 128)]
    chunks += [pl.ds(start, 256) for start in range(256, rows, 256)]
    pieces = len(chunks) + 1
    every = count * tokens
    dma = pltpu.SemaphoreType.DMA
    anywhere = pl.BlockSpec(memory_space=pl.ANY)
    in_vmem = pl.BlockSpec(memory_space=pltpu.VMEM)
    results = pl.pallas_call(
        functools.partial(kernel, bit, chips, chunks, features ** (-0.5)),
        out_shape=(
            pltpu.VMEM((1, tokens, width), BF16),
            pltpu.VMEM((1, tokens, features), BF16),
            pltpu.VMEM((1, rows, width), F32),
        ),
        in_specs=[pl.BlockSpec(memory_space=pltpu.SMEM), anywhere, anywhere, anywhere],
        out_specs=(in_vmem, in_vmem, in_vmem),
        scratch_shapes=[
            pltpu.VMEM((every, rows), BF16),
            pltpu.VMEM((every, width), BF16),
            pltpu.VMEM((rows, width), F32),
            pltpu.VMEM((rows, width), BF16),
            pltpu.VMEM((every - tokens, rows), BF16),
            pltpu.VMEM((every, width), F32),
            pltpu.VMEM((chips * tokens, width), BF16),
            pltpu.VMEM((chips * tokens, width), BF16),
            pltpu.VMEM((chips * tokens, width), BF16),
            pltpu.VMEM((chips * tokens, width), BF16),
            pltpu.VMEM((rows, width), BF16),
            pltpu.VMEM((rows, width), BF16),
            dma((3,)),
            dma((2 * count,)), dma((2 * count,)),
            dma((len(chunks) * count,)), dma((len(chunks) * count,)),
            dma((count,)), dma((count,)),
            dma((chips,)), dma((chips,)),
            dma((chips,)), dma((chips,)),
            dma((pieces,)), dma((pieces,)),
        ],
        compiler_params=pltpu.CompilerParams(
            collective_id=bit, has_side_effects=True, vmem_limit_bytes=40 * 2 ** 20),
        cost_estimate=pl.CostEstimate(
            flops=6 * every * rows * width, bytes_accessed=8 * 2 ** 20, transcendentals=0),
        name="step_bit_%d" % bit,
    )(step_index, activations, weights, cotangent)
    return pl.pallas_call(
        store_kernel,
        out_shape=tuple(jax.ShapeDtypeStruct(part.shape, part.dtype) for part in results),
        in_specs=[anywhere] * 3,
        out_specs=(anywhere, anywhere, anywhere),
        scratch_shapes=[dma((9,))],
        compiler_params=pltpu.CompilerParams(vmem_limit_bytes=2 ** 20),
        name="store",
    )(*results)


def body(count, activations, weights, cotangent, step_index):
    branches = [functools.partial(step_kernel, bit, count) for bit in range(BITS)]
    return lax.switch(step_index[0] % BITS, branches, activations, weights, cotangent, step_index)


def solution(mesh):
    split = P("rep", "fsdp", None)
    return jax.shard_map(
        functools.partial(body, mesh.shape["fsdp"]),
        mesh=mesh,
        in_specs=(split, split, split, P()),
        out_specs=(split, split, split),
        check_vma=False,
    )
```

```python
import functools

import jax
import jax.numpy as jnp
from jax import lax
from jax.experimental import pallas as pl
from jax.experimental.pallas import tpu as pltpu
from jax.sharding import PartitionSpec as P

BITS = 3
MESH = pl.DeviceIdType.MESH
BF16 = jnp.bfloat16
F32 = jnp.float32


def kernel(
    bit, chips, chunks, scale,
    step_ref, act_hbm, w_hbm, cot_hbm,
    proj_ref, ig_ref, mixed_ref,
    act, cot, w, wb, ig, part, to_sib, from_sib, to_chip, from_chip, give, take,
    local_sem, cot_send, cot_recv, act_send, act_recv, ig_send, ig_recv,
    sib_send, sib_recv, chip_send, chip_recv, give_sem, take_sem,
):
    rep, me = lax.axis_index("rep"), lax.axis_index("fsdp")
    chip, core = me // 2, me % 2
    tokens = cot_hbm.shape[1]
    rows = w_hbm.shape[1]
    slots = 2 * chips
    half = 2 ** bit
    partner = rep + half - 2 * half * ((rep // half) % 2)

    def device(ahead, other):
        return ((chip + ahead + chips) % chips) * 2 + (core + other) % 2

    def sender(slot):
        return device(-(slot // 2), slot % 2)

    def receiver(slot):
        return device(slot // 2, slot % 2)

    def to_peer(src, dst, send, recv, peer):
        return pltpu.make_async_remote_copy(
            src_ref=src, dst_ref=dst, send_sem=send, recv_sem=recv,
            device_id=(rep, peer), device_id_type=MESH,
        )

    def of(slot):
        return pl.ds(slot * tokens, tokens)

    def cols(owner):
        return pl.ds(pl.multiple_of(owner * rows, rows), rows)

    def piece(owner, c):
        start, size = chunks[c].start, chunks[c].size
        return pl.ds(pl.multiple_of(owner * rows + start, 128), size)

    load_cot = pltpu.make_async_copy(cot_hbm.at[0], cot.at[of(0)], local_sem.at[0])
    load_act = pltpu.make_async_copy(act_hbm.at[0, :, cols(me)], act.at[of(0)], local_sem.at[1])
    load_w = pltpu.make_async_copy(w_hbm.at[0], w, local_sem.at[2])
    load_cot.start()
    load_w.start()
    load_act.start()

    barrier = pltpu.get_barrier_semaphore()
    for slot in range(1, slots):
        pl.semaphore_signal(barrier, inc=1, device_id=(rep, receiver(slot)), device_id_type=MESH)
    pl.semaphore_signal(barrier, inc=1, device_id=(partner, me), device_id_type=MESH)
    pl.semaphore_wait(barrier, slots)

    far = list(range(2, slots))
    order = far + [1]
    width = w.shape[1]
    halves = [pl.ds(0, width // 2), pl.ds(width // 2, width // 2)]
    cot_copies, act_copies, ig_copies = {}, {}, {}

    def start_cot(h, src, slot, peer):
        copy = to_peer(
            src, cot.at[of(slot), halves[h]],
            cot_send.at[h * slots + slot], cot_recv.at[h * slots + slot], peer)
        copy.start()
        cot_copies[h, slot] = copy

    def send_cot(h):
        for slot in list(range(2, slots, 2)) + [1]:
            start_cot(h, cot_hbm.at[0, :, halves[h]], slot, receiver(slot))

    def take_cot(h):
        for slot in range(2, slots, 2):
            cot_copies[h, slot].wait_recv()
            start_cot(h, cot.at[of(slot), halves[h]], slot + 1, device(0, 1))

    def wait_cot(h):
        for slot in range(1, slots, 2):
            cot_copies[h, slot].wait_recv()

    def send_act(c):
        for slot in order:
            copy = to_peer(
                act_hbm.at[0, :, piece(receiver(slot), c)],
                act.at[of(slot), chunks[c]],
                act_send.at[c * slots + slot], act_recv.at[c * slots + slot], receiver(slot))
            copy.start()
            act_copies[c, slot] = copy

    def wait_act(c):
        for slot in order:
            act_copies[c, slot].wait_recv()

    def input_grad(slot):
        grad = (lax.dot_general(
            cot[of(slot), :], wb[...], (((1,), (1,)), ((), ())), preferred_element_type=F32
        ) * scale).astype(BF16)
        if slot == 0:
            ig_ref[0, :, cols(me)] = grad
        else:
            ig[of(slot - 1), :] = grad

    def send_ig(slot):
        copy = to_peer(
            ig.at[of(slot - 1)], ig_ref.at[0, :, cols(me)], ig_send.at[slot], ig_recv.at[slot], sender(slot))
        copy.start()
        ig_copies[slot] = copy

    later = [functools.partial(send_act, c) for c in range(1, len(chunks))]

    def send_next(most=1):
        for _ in range(most):
            if later:
                later.pop(0)()

    gossip = []

    def update(here, across):
        grad = lax.dot_general(
            act[:, here], cot[:, across], (((0,), (0,)), ((), ())), preferred_element_type=F32)
        new = w[here, across] - rate[:, across.start:across.start + across.size] * (grad * scale)
        mixed_ref[0, here, across] = new
        give[here, across] = new.astype(BF16)
        at = len(gossip)
        copy = pltpu.make_async_remote_copy(
            src_ref=give.at[here, across], dst_ref=take.at[here, across],
            send_sem=give_sem.at[at], recv_sem=take_sem.at[at],
            device_id=(partner, me), device_id_type=MESH,
        )
        copy.start()
        gossip.append((here, across, copy))

    def project(c):
        here = chunks[c]
        for slot in range(slots):
            term = lax.dot_general(
                act[of(slot), here], wb[here, :], (((1,), (0,)), ((), ())), preferred_element_type=F32)
            part[of(slot), :] = term if c == 0 else part[of(slot), :] + term

    send_cot(0)
    send_act(0)
    send_cot(1)

    step = jnp.full((1, width), step_ref[0], jnp.int32).astype(F32)
    rate = 0.3 / jnp.sqrt(1.0 + step / 50.0)
    load_w.wait()
    load_cot.wait()
    load_act.wait()

    take_cot(0)
    send_next()
    wait_cot(0)
    wait_act(0)
    send_next()
    update(chunks[0], halves[0])
    take_cot(1)
    send_next()
    wb[...] = w[...].astype(BF16)
    wait_cot(1)
    update(chunks[0], halves[1])

    for c in range(1, len(chunks)):
        wait_act(c)
        send_next()
        update(chunks[c], pl.ds(0, width))
        if c == 1:
            for slot in order + [0]:
                input_grad(slot)
            send_ig(1)
            later += [functools.partial(send_ig, slot) for slot in far]
            project(0)
        project(c)
    send_next(len(later))

    sib_copies = []
    for ahead in list(range(1, chips)) + [0]:
        here = pl.ds(ahead * tokens, tokens)
        to_sib[here, :] = part[of(2 * ahead + 1), :].astype(BF16)
        copy = to_peer(
            to_sib.at[here], from_sib.at[here], sib_send.at[ahead], sib_recv.at[ahead], device(0, 1))
        copy.start()
        sib_copies.append((ahead, copy))
    chip_copies = []
    for ahead, copy in sib_copies:
        here = pl.ds(ahead * tokens, tokens)
        copy.wait_recv()
        if ahead > 0:
            to_chip[here, :] = (part[of(2 * ahead), :] + from_sib[here, :].astype(F32)).astype(BF16)
            on = to_peer(
                to_chip.at[here], from_chip.at[here], chip_send.at[ahead], chip_recv.at[ahead], sender(2 * ahead))
            on.start()
            chip_copies.append((ahead, on))

    for here, across, copy in gossip:
        copy.wait_recv()
        mixed_ref[0, here, across] = 0.5 * (mixed_ref[0, here, across] + take[here, across].astype(F32))

    total = part[of(0), :] + from_sib[pl.ds(0, tokens), :].astype(F32)
    for ahead, on in chip_copies:
        on.wait_recv()
        total = total + from_chip[pl.ds(ahead * tokens, tokens), :].astype(F32)
    proj_ref[0] = (total * scale).astype(BF16)

    for copy in ig_copies.values():
        copy.wait_recv()
    for copy in list(cot_copies.values()) + list(act_copies.values()) + list(ig_copies.values()):
        copy.wait_send()
    for copy in [copy for _, copy in sib_copies + chip_copies] + [copy for _, _, copy in gossip]:
        copy.wait_send()


def pair_kernel(
    bit, half_rows, scale,
    step_ref, act_hbm, w_hbm, cot_hbm,
    proj_ref, ig_ref, mixed_ref,
    act, cot, w, ws, acc, p_out, p_in, q, pair_out, pair_in, w_in, s_out, s_in,
    plain_out, plain_in, new_out, new_in, back_out, back_in,
    local_sem, ws_send, ws_recv, p_send, p_recv, far_send, far_recv, pair_send, pair_recv,
):
    rep, me = lax.axis_index("rep"), lax.axis_index("fsdp")
    chip, core = me // 2, me % 2
    owners = [me, chip * 2 + 1 - core, (1 - chip) * 2 + core, (1 - chip) * 2 + 1 - core]
    rows, width = w.shape
    size = rows // 4
    sub = half_rows // 2
    plain = pl.ds(2 * half_rows, rows - 2 * half_rows)
    side = (rep // 2 ** bit) % 2
    partner = rep + 2 ** bit - 2 * 2 ** bit * side
    mine, theirs = side * half_rows, (1 - side) * half_rows
    started = []

    def go(src, dst, send, recv, at, device):
        copy = pltpu.make_async_remote_copy(
            src_ref=src, dst_ref=dst, send_sem=send.at[at], recv_sem=recv.at[at],
            device_id=device, device_id_type=MESH,
        )
        copy.start()
        started.append(copy)
        return copy

    core_id, far_id, pair_id = (rep, owners[1]), (rep, owners[2]), (partner, me)

    def part(start, count):
        return pl.ds(pl.multiple_of(start, 16), count)

    def lanes(slot, k):
        return pl.ds(pl.multiple_of(owners[slot] * rows + k * size, 128), size)

    load_w = pltpu.make_async_copy(w_hbm.at[0], w, local_sem.at[0])
    load_cot = pltpu.make_async_copy(cot_hbm.at[0], cot, local_sem.at[1])
    load_act = pltpu.make_async_copy(act_hbm.at[0], act, local_sem.at[2])
    load_w.start()
    load_cot.start()
    load_act.start()

    barrier = pltpu.get_barrier_semaphore()
    for device in (core_id, far_id, pair_id):
        pl.semaphore_signal(barrier, inc=1, device_id=device, device_id_type=MESH)
    load_w.wait()
    ws[pl.ds(0, rows), :] = w[...].astype(BF16)
    pl.semaphore_wait(barrier, 3)

    def send_w(slot, k):
        source = 2 if slot == 3 else 0
        return go(
            ws.at[pl.ds(source * rows + k * size, size)], ws.at[pl.ds(slot * rows + k * size, size)],
            ws_send, ws_recv, slot * 4 + k, far_id if slot == 2 else core_id)

    w_copies = {(2, k): send_w(2, k) for k in (0, 1)}
    w_pair = go(ws.at[part(theirs, half_rows)], w_in, pair_send, pair_recv, 0, pair_id)
    load_cot.wait()
    load_act.wait()

    def term(slot, k):
        return lax.dot_general(
            act[:, lanes(slot, k)], cot[...], (((0,), (0,)), ((), ())), preferred_element_type=F32)

    p_copies = {}
    for k in range(4):
        for at, slot in ((1, 3), (0, 1)):
            here = pl.ds(at * rows + k * size, size)
            p_out[here, :] = term(slot, k).astype(BF16)
            p_copies[at, k] = go(p_out.at[here], p_in.at[here], p_send, p_recv, at * 4 + k, core_id)
    for k in range(4):
        w_copies[1, k] = send_w(1, k)
    for k in range(4):
        for at, slot in ((1, 2), (0, 0)):
            here = pl.ds(at * rows + k * size, size)
            own = term(slot, k)
            p_copies[at, k].wait_recv()
            q[here, :] = own + p_in[here, :].astype(F32)

    pair_copies = {}
    for at in (1, 0):
        for j in range(2):
            here = pl.ds(at * half_rows + j * sub, sub)
            pair_out[here, :] = q[part(at * rows + theirs + j * sub, sub), :].astype(BF16)
            pair_copies[at, j] = go(
                pair_out.at[here], pair_in.at[here], pair_send, pair_recv, 1 + at * 2 + j, pair_id)
    plain_out[...] = q[pl.ds(rows + 2 * half_rows, rows - 2 * half_rows), :].astype(BF16)
    plain_copy = go(plain_out, plain_in, far_send, far_recv, 0, far_id)

    step = jnp.full((1, width), step_ref[0], jnp.int32).astype(F32)
    rate = 0.3 / jnp.sqrt(1.0 + step / 50.0) * scale

    def multiply(slot, k):
        block = ws[pl.ds(slot * rows + k * size, size), :]
        ig_ref[0, :, lanes(slot, k)] = (lax.dot_general(
            cot[...], block, (((1,), (1,)), ((), ())), preferred_element_type=F32) * scale).astype(BF16)
        out = jnp.dot(act[:, lanes(slot, k)], block, preferred_element_type=F32)
        acc[...] = out if (slot, k) == (0, 0) else acc[...] + out

    def arrive(k):
        w_copies[2, k].wait_recv()
        w_copies[3, k] = send_w(3, k)

    for k in range(4):
        multiply(0, k)
    arrive(0)
    w_copies[2, 2] = send_w(2, 2)
    for k in range(4):
        w_copies[1, k].wait_recv()
        multiply(1, k)

    far_copies = []
    for j in range(2):
        here = pl.ds(j * sub, sub)
        pair_copies[1, j].wait_recv()
        s_out[here, :] = (
            q[part(rows + mine + j * sub, sub), :] + pair_in[pl.ds(half_rows + j * sub, sub), :].astype(F32)
        ).astype(BF16)
        far_copies.append(go(s_out.at[here], s_in.at[here], far_send, far_recv, 1 + j, far_id))

    arrive(1)
    w_copies[2, 3] = send_w(2, 3)
    multiply(2, 0)
    multiply(2, 1)

    plain_copy.wait_recv()
    new = w[plain, :] - rate * (q[plain, :] + plain_in[...].astype(F32))
    mixed_ref[0, plain, :] = new
    new_out[...] = new.astype(BF16)
    new_copy = go(new_out, new_in, pair_send, pair_recv, 5, pair_id)

    w_pair.wait_recv()
    back_copies = []
    for j in range(2):
        here = pl.ds(j * sub, sub)
        there = part(mine + j * sub, sub)
        pair_copies[0, j].wait_recv()
        far_copies[j].wait_recv()
        grad = (q[there, :] + pair_in[here, :].astype(F32)) + s_in[here, :].astype(F32)
        mean = 0.5 * ((w[there, :] + w_in[here, :].astype(F32)) - rate * grad)
        mixed_ref[0, there, :] = mean
        back_out[here, :] = mean.astype(BF16)
        back_copies.append(go(back_out.at[here], back_in.at[here], pair_send, pair_recv, 6 + j, pair_id))

    arrive(2)
    multiply(2, 2)
    for k in (0, 1):
        w_copies[3, k].wait_recv()
        multiply(3, k)
    arrive(3)
    multiply(2, 3)
    w_copies[3, 2].wait_recv()
    multiply(3, 2)

    new_copy.wait_recv()
    mixed_ref[0, plain, :] = 0.5 * (mixed_ref[0, plain, :] + new_in[...].astype(F32))
    w_copies[3, 3].wait_recv()
    multiply(3, 3)
    proj_ref[0] = (acc[...] * scale).astype(BF16)
    for j in range(2):
        back_copies[j].wait_recv()
        mixed_ref[0, part(theirs + j * sub, sub), :] = back_in[pl.ds(j * sub, sub), :].astype(F32)
    for copy in started:
        copy.wait_send()


def store_kernel(proj_ref, ig_ref, mixed_ref, proj_hbm, ig_hbm, mixed_hbm, sem):
    copies = [pltpu.make_async_copy(proj_ref, proj_hbm, sem.at[0])]
    for src, dst in ((ig_ref, ig_hbm), (mixed_ref, mixed_hbm)):
        size = src.shape[1] // 4
        for c in range(4):
            here = pl.ds(c * size, size)
            copies.append(pltpu.make_async_copy(src.at[0, here], dst.at[0, here], sem.at[len(copies)]))
    for copy in copies:
        copy.start()
    for copy in copies:
        copy.wait()


def step_kernel(bit, count, activations, weights, cotangent, step_index):
    tokens, features = activations.shape[1:]
    rows, width = weights.shape[1:]
    chips = count // 2
    chunks = [pl.ds(start, 128) for start in range(0, min(rows, 256), 128)]
    chunks += [pl.ds(start, 256) for start in range(256, rows, 256)]
    pieces = len(chunks) + 1
    every = count * tokens
    dma = pltpu.SemaphoreType.DMA
    anywhere = pl.BlockSpec(memory_space=pl.ANY)
    in_vmem = pl.BlockSpec(memory_space=pltpu.VMEM)
    half_rows = rows * 5 // 16
    if chips == 2 and bit < 2 and rows % 1024 == 0:
        run = functools.partial(pair_kernel, bit, half_rows, features ** (-0.5))

        def block(count):
            return pltpu.VMEM((count, width), BF16)

        scratch = [
            pltpu.VMEM((tokens, features), BF16), block(tokens),
            pltpu.VMEM((rows, width), F32), block(4 * rows), pltpu.VMEM((tokens, width), F32),
            block(2 * rows), block(2 * rows), pltpu.VMEM((2 * rows, width), F32),
            block(2 * half_rows), block(2 * half_rows), block(half_rows),
            block(half_rows), block(half_rows),
            block(rows - 2 * half_rows), block(rows - 2 * half_rows),
            block(rows - 2 * half_rows), block(rows - 2 * half_rows),
            block(half_rows), block(half_rows),
            dma((3,)), dma((16,)), dma((16,)), dma((8,)), dma((8,)),
            dma((3,)), dma((3,)), dma((8,)), dma((8,)),
        ]
    else:
        run = functools.partial(kernel, bit, chips, chunks, features ** (-0.5))
        scratch = [
            pltpu.VMEM((every, rows), BF16),
            pltpu.VMEM((every, width), BF16),
            pltpu.VMEM((rows, width), F32),
            pltpu.VMEM((rows, width), BF16),
            pltpu.VMEM((every - tokens, rows), BF16),
            pltpu.VMEM((every, width), F32),
            pltpu.VMEM((chips * tokens, width), BF16),
            pltpu.VMEM((chips * tokens, width), BF16),
            pltpu.VMEM((chips * tokens, width), BF16),
            pltpu.VMEM((chips * tokens, width), BF16),
            pltpu.VMEM((rows, width), BF16),
            pltpu.VMEM((rows, width), BF16),
            dma((3,)),
            dma((2 * count,)), dma((2 * count,)),
            dma((len(chunks) * count,)), dma((len(chunks) * count,)),
            dma((count,)), dma((count,)),
            dma((chips,)), dma((chips,)),
            dma((chips,)), dma((chips,)),
            dma((pieces,)), dma((pieces,)),
        ]
    results = pl.pallas_call(
        run,
        out_shape=(
            pltpu.VMEM((1, tokens, width), BF16),
            pltpu.VMEM((1, tokens, features), BF16),
            pltpu.VMEM((1, rows, width), F32),
        ),
        in_specs=[pl.BlockSpec(memory_space=pltpu.SMEM), anywhere, anywhere, anywhere],
        out_specs=(in_vmem, in_vmem, in_vmem),
        scratch_shapes=scratch,
        compiler_params=pltpu.CompilerParams(
            collective_id=bit, has_side_effects=True, vmem_limit_bytes=40 * 2 ** 20),
        cost_estimate=pl.CostEstimate(
            flops=6 * every * rows * width, bytes_accessed=8 * 2 ** 20, transcendentals=0),
        name="step_bit_%d" % bit,
    )(step_index, activations, weights, cotangent)
    return pl.pallas_call(
        store_kernel,
        out_shape=tuple(jax.ShapeDtypeStruct(part.shape, part.dtype) for part in results),
        in_specs=[anywhere] * 3,
        out_specs=(anywhere, anywhere, anywhere),
        scratch_shapes=[dma((9,))],
        compiler_params=pltpu.CompilerParams(vmem_limit_bytes=2 ** 20),
        name="store",
    )(*results)


def body(count, activations, weights, cotangent, step_index):
    branches = [functools.partial(step_kernel, bit, count) for bit in range(BITS)]
    return lax.switch(step_index[0] % BITS, branches, activations, weights, cotangent, step_index)


def solution(mesh):
    split = P("rep", "fsdp", None)
    return jax.shard_map(
        functools.partial(body, mesh.shape["fsdp"]),
        mesh=mesh,
        in_specs=(split, split, split, P()),
        out_specs=(split, split, split),
        check_vma=False,
    )
```

```python
import functools

import jax
import jax.numpy as jnp
from jax import lax
from jax.experimental import pallas as pl
from jax.experimental.pallas import tpu as pltpu
from jax.sharding import PartitionSpec as P

BITS = 3
MESH = pl.DeviceIdType.MESH
BF16 = jnp.bfloat16
F32 = jnp.float32


def kernel(
    bit, chips, chunks, scale,
    step_ref, act_hbm, w_hbm, cot_hbm,
    proj_ref, ig_ref, mixed_ref,
    act, cot, w, wb, ig, part, to_sib, from_sib, to_chip, from_chip, give, take,
    local_sem, cot_send, cot_recv, act_send, act_recv, ig_send, ig_recv,
    sib_send, sib_recv, chip_send, chip_recv, give_sem, take_sem,
):
    rep, me = lax.axis_index("rep"), lax.axis_index("fsdp")
    chip, core = me // 2, me % 2
    tokens = cot_hbm.shape[1]
    rows = w_hbm.shape[1]
    slots = 2 * chips
    half = 2 ** bit
    partner = rep + half - 2 * half * ((rep // half) % 2)

    def device(ahead, other):
        return ((chip + ahead + chips) % chips) * 2 + (core + other) % 2

    def sender(slot):
        return device(-(slot // 2), slot % 2)

    def receiver(slot):
        return device(slot // 2, slot % 2)

    def to_peer(src, dst, send, recv, peer):
        return pltpu.make_async_remote_copy(
            src_ref=src, dst_ref=dst, send_sem=send, recv_sem=recv,
            device_id=(rep, peer), device_id_type=MESH,
        )

    def of(slot):
        return pl.ds(slot * tokens, tokens)

    def cols(owner):
        return pl.ds(pl.multiple_of(owner * rows, rows), rows)

    def piece(owner, c):
        start, size = chunks[c].start, chunks[c].size
        return pl.ds(pl.multiple_of(owner * rows + start, 128), size)

    load_cot = pltpu.make_async_copy(cot_hbm.at[0], cot.at[of(0)], local_sem.at[0])
    load_act = pltpu.make_async_copy(act_hbm.at[0, :, cols(me)], act.at[of(0)], local_sem.at[1])
    load_w = pltpu.make_async_copy(w_hbm.at[0], w, local_sem.at[2])
    load_cot.start()
    load_w.start()
    load_act.start()

    barrier = pltpu.get_barrier_semaphore()
    for slot in range(1, slots):
        pl.semaphore_signal(barrier, inc=1, device_id=(rep, receiver(slot)), device_id_type=MESH)
    pl.semaphore_signal(barrier, inc=1, device_id=(partner, me), device_id_type=MESH)
    pl.semaphore_wait(barrier, slots)

    far = list(range(2, slots))
    order = far + [1]
    width = w.shape[1]
    halves = [pl.ds(0, width // 2), pl.ds(width // 2, width // 2)]
    cot_copies, act_copies, ig_copies = {}, {}, {}

    def start_cot(h, src, slot, peer):
        copy = to_peer(
            src, cot.at[of(slot), halves[h]],
            cot_send.at[h * slots + slot], cot_recv.at[h * slots + slot], peer)
        copy.start()
        cot_copies[h, slot] = copy

    def send_cot(h):
        for slot in list(range(2, slots, 2)) + [1]:
            start_cot(h, cot_hbm.at[0, :, halves[h]], slot, receiver(slot))

    def take_cot(h):
        for slot in range(2, slots, 2):
            cot_copies[h, slot].wait_recv()
            start_cot(h, cot.at[of(slot), halves[h]], slot + 1, device(0, 1))

    def wait_cot(h):
        for slot in range(1, slots, 2):
            cot_copies[h, slot].wait_recv()

    def send_act(c):
        for slot in order:
            copy = to_peer(
                act_hbm.at[0, :, piece(receiver(slot), c)],
                act.at[of(slot), chunks[c]],
                act_send.at[c * slots + slot], act_recv.at[c * slots + slot], receiver(slot))
            copy.start()
            act_copies[c, slot] = copy

    def wait_act(c):
        for slot in order:
            act_copies[c, slot].wait_recv()

    def input_grad(slot):
        grad = (lax.dot_general(
            cot[of(slot), :], wb[...], (((1,), (1,)), ((), ())), preferred_element_type=F32
        ) * scale).astype(BF16)
        if slot == 0:
            ig_ref[0, :, cols(me)] = grad
        else:
            ig[of(slot - 1), :] = grad

    def send_ig(slot):
        copy = to_peer(
            ig.at[of(slot - 1)], ig_ref.at[0, :, cols(me)], ig_send.at[slot], ig_recv.at[slot], sender(slot))
        copy.start()
        ig_copies[slot] = copy

    later = [functools.partial(send_act, c) for c in range(1, len(chunks))]

    def send_next(most=1):
        for _ in range(most):
            if later:
                later.pop(0)()

    gossip = []

    def update(here, across):
        grad = lax.dot_general(
            act[:, here], cot[:, across], (((0,), (0,)), ((), ())), preferred_element_type=F32)
        new = w[here, across] - rate[:, across.start:across.start + across.size] * (grad * scale)
        mixed_ref[0, here, across] = new
        give[here, across] = new.astype(BF16)
        at = len(gossip)
        copy = pltpu.make_async_remote_copy(
            src_ref=give.at[here, across], dst_ref=take.at[here, across],
            send_sem=give_sem.at[at], recv_sem=take_sem.at[at],
            device_id=(partner, me), device_id_type=MESH,
        )
        copy.start()
        gossip.append((here, across, copy))

    def project(c):
        here = chunks[c]
        for slot in range(slots):
            term = lax.dot_general(
                act[of(slot), here], wb[here, :], (((1,), (0,)), ((), ())), preferred_element_type=F32)
            part[of(slot), :] = term if c == 0 else part[of(slot), :] + term

    send_cot(0)
    send_act(0)
    send_cot(1)

    step = jnp.full((1, width), step_ref[0], jnp.int32).astype(F32)
    rate = 0.3 / jnp.sqrt(1.0 + step / 50.0)
    load_w.wait()
    load_cot.wait()
    load_act.wait()

    take_cot(0)
    send_next()
    wait_cot(0)
    wait_act(0)
    send_next()
    update(chunks[0], halves[0])
    take_cot(1)
    send_next()
    wb[...] = w[...].astype(BF16)
    wait_cot(1)
    update(chunks[0], halves[1])

    busy = min(2, len(chunks) - 1)
    for c in range(1, len(chunks)):
        wait_act(c)
        send_next()
        update(chunks[c], pl.ds(0, width))
        if c == busy:
            for slot in order + [0]:
                input_grad(slot)
            send_ig(1)
            later += [functools.partial(send_ig, slot) for slot in far]
            for before in range(c):
                project(before)
        if c >= busy:
            project(c)
    send_next(len(later))

    sib_copies = []
    for ahead in list(range(1, chips)) + [0]:
        here = pl.ds(ahead * tokens, tokens)
        to_sib[here, :] = part[of(2 * ahead + 1), :].astype(BF16)
        copy = to_peer(
            to_sib.at[here], from_sib.at[here], sib_send.at[ahead], sib_recv.at[ahead], device(0, 1))
        copy.start()
        sib_copies.append((ahead, copy))
    chip_copies = []
    for ahead, copy in sib_copies:
        here = pl.ds(ahead * tokens, tokens)
        copy.wait_recv()
        if ahead > 0:
            to_chip[here, :] = (part[of(2 * ahead), :] + from_sib[here, :].astype(F32)).astype(BF16)
            on = to_peer(
                to_chip.at[here], from_chip.at[here], chip_send.at[ahead], chip_recv.at[ahead], sender(2 * ahead))
            on.start()
            chip_copies.append((ahead, on))

    for here, across, copy in gossip:
        copy.wait_recv()
        mixed_ref[0, here, across] = 0.5 * (mixed_ref[0, here, across] + take[here, across].astype(F32))

    total = part[of(0), :] + from_sib[pl.ds(0, tokens), :].astype(F32)
    for ahead, on in chip_copies:
        on.wait_recv()
        total = total + from_chip[pl.ds(ahead * tokens, tokens), :].astype(F32)
    proj_ref[0] = (total * scale).astype(BF16)

    for copy in ig_copies.values():
        copy.wait_recv()
    for copy in list(cot_copies.values()) + list(act_copies.values()) + list(ig_copies.values()):
        copy.wait_send()
    for copy in [copy for _, copy in sib_copies + chip_copies] + [copy for _, _, copy in gossip]:
        copy.wait_send()


def pair_kernel(
    bit, half_rows, chunks, scale,
    step_ref, act_hbm, w_hbm, cot_hbm,
    proj_ref, ig_ref, mixed_ref,
    act, cot, w, ws, acc, p_out, p_in, q, pair_out, pair_in, w_in, s_out, s_in,
    plain_out, plain_in, new_out, new_in, back_out, back_in,
    local_sem, ws_send, ws_recv, p_send, p_recv, far_send, far_recv, pair_send, pair_recv,
):
    rep, me = lax.axis_index("rep"), lax.axis_index("fsdp")
    chip, core = me // 2, me % 2
    owners = [me, chip * 2 + 1 - core, (1 - chip) * 2 + core, (1 - chip) * 2 + 1 - core]
    rows, width = w.shape
    size = rows // 4
    sub = half_rows // 2
    plain = pl.ds(2 * half_rows, rows - 2 * half_rows)
    side = (rep // 2 ** bit) % 2
    partner = rep + 2 ** bit - 2 * 2 ** bit * side
    mine, theirs = side * half_rows, (1 - side) * half_rows
    started = []

    def go(src, dst, send, recv, at, device):
        copy = pltpu.make_async_remote_copy(
            src_ref=src, dst_ref=dst, send_sem=send.at[at], recv_sem=recv.at[at],
            device_id=device, device_id_type=MESH,
        )
        copy.start()
        started.append(copy)
        return copy

    core_id, far_id, pair_id = (rep, owners[1]), (rep, owners[2]), (partner, me)

    def part(start, count):
        return pl.ds(pl.multiple_of(start, 16), count)

    def lanes(slot, here):
        return pl.ds(pl.multiple_of(owners[slot] * rows + here.start, 128), here.size)

    def rows_of(slot, here):
        return pl.ds(slot * rows + here.start, here.size)

    load_w = pltpu.make_async_copy(w_hbm.at[0], w, local_sem.at[0])
    load_cot = pltpu.make_async_copy(cot_hbm.at[0], cot, local_sem.at[1])
    load_act = pltpu.make_async_copy(act_hbm.at[0], act, local_sem.at[2])
    load_w.start()
    load_cot.start()
    load_act.start()

    barrier = pltpu.get_barrier_semaphore()
    for device in (core_id, far_id, pair_id):
        pl.semaphore_signal(barrier, inc=1, device_id=device, device_id_type=MESH)
    load_w.wait()
    ws[pl.ds(0, rows), :] = w[...].astype(BF16)
    pl.semaphore_wait(barrier, 3)

    w_copies = {}

    def send_w(slot, k):
        source = 2 if slot == 3 else 0
        w_copies[slot, k] = go(
            ws.at[rows_of(source, chunks[k])], ws.at[rows_of(slot, chunks[k])],
            ws_send, ws_recv, slot * len(chunks) + k, far_id if slot == 2 else core_id)

    def send_w_pair(j):
        return go(
            ws.at[part(theirs + j * sub, sub)], w_in.at[pl.ds(j * sub, sub)],
            pair_send, pair_recv, 7 + j, pair_id)

    send_w(2, 0)
    w_pair = [send_w_pair(0)]
    load_cot.wait()
    load_act.wait()

    def term(slot, k):
        return lax.dot_general(
            act[:, lanes(slot, pl.ds(k * size, size))], cot[...],
            (((0,), (0,)), ((), ())), preferred_element_type=F32)

    def send_terms(at, slot):
        copies = []
        for k in range(4):
            here = pl.ds(at * rows + k * size, size)
            p_out[here, :] = term(slot, k).astype(BF16)
            copies.append(go(p_out.at[here], p_in.at[here], p_send, p_recv, at * 4 + k, core_id))
        return copies

    def add_terms(at, slot, copies):
        for k in range(4):
            here = pl.ds(at * rows + k * size, size)
            own = term(slot, k)
            copies[k].wait_recv()
            q[here, :] = own + p_in[here, :].astype(F32)

    pair_copies = {}

    def send_pair(at, j):
        here = pl.ds(at * half_rows + j * sub, sub)
        pair_out[here, :] = q[part(at * rows + theirs + j * sub, sub), :].astype(BF16)
        pair_copies[at, j] = go(
            pair_out.at[here], pair_in.at[here], pair_send, pair_recv, at * 2 + j, pair_id)

    add_terms(1, 2, send_terms(1, 3))
    send_pair(1, 0)
    send_pair(1, 1)
    plain_out[...] = q[pl.ds(rows + 2 * half_rows, rows - 2 * half_rows), :].astype(BF16)
    plain_copy = go(plain_out, plain_in, far_send, far_recv, 0, far_id)
    near = send_terms(0, 1)
    for k in range(len(chunks)):
        send_w(1, k)
    add_terms(0, 0, near)

    step = jnp.full((1, width), step_ref[0], jnp.int32).astype(F32)
    rate = 0.3 / jnp.sqrt(1.0 + step / 50.0) * scale

    def multiply(slot, k):
        block = ws[rows_of(slot, chunks[k]), :]
        across = lanes(slot, chunks[k])
        ig_ref[0, :, across] = (lax.dot_general(
            cot[...], block, (((1,), (1,)), ((), ())), preferred_element_type=F32) * scale).astype(BF16)
        out = jnp.dot(act[:, across], block, preferred_element_type=F32)
        acc[...] = out if (slot, k) == (0, 0) else acc[...] + out

    def arrive(k):
        w_copies[2, k].wait_recv()
        send_w(3, k)

    def forwarded(k):
        w_copies[3, k].wait_recv()
        multiply(3, k)

    last = len(chunks) - 1
    multiply(0, 0)
    far_copies = []
    for j in range(2):
        here = pl.ds(j * sub, sub)
        pair_copies[1, j].wait_recv()
        s_out[here, :] = (
            q[part(rows + mine + j * sub, sub), :] + pair_in[pl.ds(half_rows + j * sub, sub), :].astype(F32)
        ).astype(BF16)
        far_copies.append(go(s_out.at[here], s_in.at[here], far_send, far_recv, 1 + j, far_id))
        send_pair(0, j)
    w_pair.append(send_w_pair(1))
    send_w(2, 1)
    arrive(0)
    for k in range(1, len(chunks)):
        multiply(0, k)
    multiply(2, 0)

    plain_copy.wait_recv()
    send_w(2, 2)
    new = w[plain, :] - rate * (q[plain, :] + plain_in[...].astype(F32))
    mixed_ref[0, plain, :] = new
    new_out[...] = new.astype(BF16)
    new_copy = go(new_out, new_in, pair_send, pair_recv, 4, pair_id)
    for k in range(len(chunks)):
        w_copies[1, k].wait_recv()
        multiply(1, k)
    forwarded(0)

    back_copies = []
    for j in range(2):
        here = pl.ds(j * sub, sub)
        there = part(mine + j * sub, sub)
        w_pair[j].wait_recv()
        pair_copies[0, j].wait_recv()
        far_copies[j].wait_recv()
        if j == 0:
            for k in range(3, len(chunks)):
                send_w(2, k)
        grad = (q[there, :] + pair_in[here, :].astype(F32)) + s_in[here, :].astype(F32)
        mean = 0.5 * ((w[there, :] + w_in[here, :].astype(F32)) - rate * grad)
        mixed_ref[0, there, :] = mean
        back_out[here, :] = mean.astype(BF16)
        back_copies.append(go(back_out.at[here], back_in.at[here], pair_send, pair_recv, 5 + j, pair_id))

    for k in range(1, last):
        arrive(k)
        multiply(2, k)
        if k > 1:
            forwarded(k - 1)
    new_copy.wait_recv()
    mixed_ref[0, plain, :] = 0.5 * (mixed_ref[0, plain, :] + new_in[...].astype(F32))
    arrive(last)
    forwarded(last - 1)
    multiply(2, last)
    for j in range(2):
        back_copies[j].wait_recv()
        mixed_ref[0, part(theirs + j * sub, sub), :] = back_in[pl.ds(j * sub, sub), :].astype(F32)
    forwarded(last)
    proj_ref[0] = (acc[...] * scale).astype(BF16)
    for copy in started:
        copy.wait_send()


def store_kernel(proj_ref, ig_ref, mixed_ref, proj_hbm, ig_hbm, mixed_hbm, sem):
    copies = [pltpu.make_async_copy(proj_ref, proj_hbm, sem.at[0])]
    for src, dst in ((ig_ref, ig_hbm), (mixed_ref, mixed_hbm)):
        size = src.shape[1] // 4
        for c in range(4):
            here = pl.ds(c * size, size)
            copies.append(pltpu.make_async_copy(src.at[0, here], dst.at[0, here], sem.at[len(copies)]))
    for copy in copies:
        copy.start()
    for copy in copies:
        copy.wait()


def step_kernel(bit, count, activations, weights, cotangent, step_index):
    tokens, features = activations.shape[1:]
    rows, width = weights.shape[1:]
    chips = count // 2
    chunks = [pl.ds(start, 128) for start in range(0, min(rows, 256), 128)]
    chunks += [pl.ds(start, 256) for start in range(256, rows, 256)]
    pieces = len(chunks) + 1
    every = count * tokens
    dma = pltpu.SemaphoreType.DMA
    anywhere = pl.BlockSpec(memory_space=pl.ANY)
    in_vmem = pl.BlockSpec(memory_space=pltpu.VMEM)
    half_rows = rows * 5 // 16
    if chips == 2 and bit < 2 and rows % 1024 == 0:
        part = rows // 8
        blocks = [pl.ds(2 * k * part, 2 * part) for k in range(3)] + [pl.ds(k * part, part) for k in (6, 7)]
        run = functools.partial(pair_kernel, bit, half_rows, blocks, features ** (-0.5))

        def block(count):
            return pltpu.VMEM((count, width), BF16)

        scratch = [
            pltpu.VMEM((tokens, features), BF16), block(tokens),
            pltpu.VMEM((rows, width), F32), block(4 * rows), pltpu.VMEM((tokens, width), F32),
            block(2 * rows), block(2 * rows), pltpu.VMEM((2 * rows, width), F32),
            block(2 * half_rows), block(2 * half_rows), block(half_rows),
            block(half_rows), block(half_rows),
            block(rows - 2 * half_rows), block(rows - 2 * half_rows),
            block(rows - 2 * half_rows), block(rows - 2 * half_rows),
            block(half_rows), block(half_rows),
            dma((3,)), dma((4 * len(blocks),)), dma((4 * len(blocks),)), dma((8,)), dma((8,)),
            dma((3,)), dma((3,)), dma((9,)), dma((9,)),
        ]
    else:
        run = functools.partial(kernel, bit, chips, chunks, features ** (-0.5))
        scratch = [
            pltpu.VMEM((every, rows), BF16),
            pltpu.VMEM((every, width), BF16),
            pltpu.VMEM((rows, width), F32),
            pltpu.VMEM((rows, width), BF16),
            pltpu.VMEM((every - tokens, rows), BF16),
            pltpu.VMEM((every, width), F32),
            pltpu.VMEM((chips * tokens, width), BF16),
            pltpu.VMEM((chips * tokens, width), BF16),
            pltpu.VMEM((chips * tokens, width), BF16),
            pltpu.VMEM((chips * tokens, width), BF16),
            pltpu.VMEM((rows, width), BF16),
            pltpu.VMEM((rows, width), BF16),
            dma((3,)),
            dma((2 * count,)), dma((2 * count,)),
            dma((len(chunks) * count,)), dma((len(chunks) * count,)),
            dma((count,)), dma((count,)),
            dma((chips,)), dma((chips,)),
            dma((chips,)), dma((chips,)),
            dma((pieces,)), dma((pieces,)),
        ]
    results = pl.pallas_call(
        run,
        out_shape=(
            pltpu.VMEM((1, tokens, width), BF16),
            pltpu.VMEM((1, tokens, features), BF16),
            pltpu.VMEM((1, rows, width), F32),
        ),
        in_specs=[pl.BlockSpec(memory_space=pltpu.SMEM), anywhere, anywhere, anywhere],
        out_specs=(in_vmem, in_vmem, in_vmem),
        scratch_shapes=scratch,
        compiler_params=pltpu.CompilerParams(
            collective_id=bit, has_side_effects=True, vmem_limit_bytes=40 * 2 ** 20),
        cost_estimate=pl.CostEstimate(
            flops=6 * every * rows * width, bytes_accessed=8 * 2 ** 20, transcendentals=0),
        name="step_bit_%d" % bit,
    )(step_index, activations, weights, cotangent)
    return pl.pallas_call(
        store_kernel,
        out_shape=tuple(jax.ShapeDtypeStruct(part.shape, part.dtype) for part in results),
        in_specs=[anywhere] * 3,
        out_specs=(anywhere, anywhere, anywhere),
        scratch_shapes=[dma((9,))],
        compiler_params=pltpu.CompilerParams(vmem_limit_bytes=2 ** 20),
        name="store",
    )(*results)


def body(count, activations, weights, cotangent, step_index):
    branches = [functools.partial(step_kernel, bit, count) for bit in range(BITS)]
    return lax.switch(step_index[0] % BITS, branches, activations, weights, cotangent, step_index)


def solution(mesh):
    split = P("rep", "fsdp", None)
    return jax.shard_map(
        functools.partial(body, mesh.shape["fsdp"]),
        mesh=mesh,
        in_specs=(split, split, split, P()),
        out_specs=(split, split, split),
        check_vma=False,
    )
```

```python
import functools

import jax
import jax.numpy as jnp
from jax import lax
from jax.experimental import pallas as pl
from jax.experimental.pallas import tpu as pltpu
from jax.sharding import PartitionSpec as P

BITS = 3
MESH = pl.DeviceIdType.MESH
BF16 = jnp.bfloat16
F32 = jnp.float32


def kernel(
    bit, chips, chunks, scale,
    step_hbm, act_hbm, w_hbm, cot_hbm,
    proj_ref, ig_ref, mixed_ref,
    act, cot, w, wb, ig, part, to_sib, from_sib, to_chip, from_chip, give, take, step_ref,
    local_sem, cot_send, cot_recv, act_send, act_recv, ig_send, ig_recv,
    sib_send, sib_recv, chip_send, chip_recv, give_sem, take_sem,
):
    rep, me = lax.axis_index("rep"), lax.axis_index("fsdp")
    chip, core = me // 2, me % 2
    tokens = cot_hbm.shape[1]
    rows = w_hbm.shape[1]
    slots = 2 * chips
    half = 2 ** bit
    partner = rep + half - 2 * half * ((rep // half) % 2)

    def device(ahead, other):
        return ((chip + ahead + chips) % chips) * 2 + (core + other) % 2

    def sender(slot):
        return device(-(slot // 2), slot % 2)

    def receiver(slot):
        return device(slot // 2, slot % 2)

    def to_peer(src, dst, send, recv, peer):
        return pltpu.make_async_remote_copy(
            src_ref=src, dst_ref=dst, send_sem=send, recv_sem=recv,
            device_id=(rep, peer), device_id_type=MESH,
        )

    def of(slot):
        return pl.ds(slot * tokens, tokens)

    def cols(owner):
        return pl.ds(pl.multiple_of(owner * rows, rows), rows)

    def piece(owner, c):
        start, size = chunks[c].start, chunks[c].size
        return pl.ds(pl.multiple_of(owner * rows + start, 128), size)

    load_cot = pltpu.make_async_copy(cot_hbm.at[0], cot.at[of(0)], local_sem.at[0])
    load_act = pltpu.make_async_copy(act_hbm.at[0, :, cols(me)], act.at[of(0)], local_sem.at[1])
    load_w = pltpu.make_async_copy(w_hbm.at[0], w, local_sem.at[2])
    load_step = pltpu.make_async_copy(step_hbm, step_ref, local_sem.at[3])
    load_cot.start()
    load_w.start()
    load_act.start()
    load_step.start()

    barrier = pltpu.get_barrier_semaphore()
    for slot in range(1, slots):
        pl.semaphore_signal(barrier, inc=1, device_id=(rep, receiver(slot)), device_id_type=MESH)
    pl.semaphore_signal(barrier, inc=1, device_id=(partner, me), device_id_type=MESH)
    pl.semaphore_wait(barrier, slots)

    far = list(range(2, slots))
    order = far + [1]
    width = w.shape[1]
    halves = [pl.ds(0, width // 2), pl.ds(width // 2, width // 2)]
    cot_copies, act_copies, ig_copies = {}, {}, {}

    def start_cot(h, src, slot, peer):
        copy = to_peer(
            src, cot.at[of(slot), halves[h]],
            cot_send.at[h * slots + slot], cot_recv.at[h * slots + slot], peer)
        copy.start()
        cot_copies[h, slot] = copy

    def send_cot(h):
        for slot in list(range(2, slots, 2)) + [1]:
            start_cot(h, cot_hbm.at[0, :, halves[h]], slot, receiver(slot))

    def take_cot(h):
        for slot in range(2, slots, 2):
            cot_copies[h, slot].wait_recv()
            start_cot(h, cot.at[of(slot), halves[h]], slot + 1, device(0, 1))

    def wait_cot(h):
        for slot in range(1, slots, 2):
            cot_copies[h, slot].wait_recv()

    def send_act(c):
        for slot in order:
            copy = to_peer(
                act_hbm.at[0, :, piece(receiver(slot), c)],
                act.at[of(slot), chunks[c]],
                act_send.at[c * slots + slot], act_recv.at[c * slots + slot], receiver(slot))
            copy.start()
            act_copies[c, slot] = copy

    def wait_act(c):
        for slot in order:
            act_copies[c, slot].wait_recv()

    def input_grad(slot):
        grad = (lax.dot_general(
            cot[of(slot), :], wb[...], (((1,), (1,)), ((), ())), preferred_element_type=F32
        ) * scale).astype(BF16)
        if slot == 0:
            ig_ref[0, :, cols(me)] = grad
        else:
            ig[of(slot - 1), :] = grad

    def send_ig(slot):
        copy = to_peer(
            ig.at[of(slot - 1)], ig_ref.at[0, :, cols(me)], ig_send.at[slot], ig_recv.at[slot], sender(slot))
        copy.start()
        ig_copies[slot] = copy

    later = [functools.partial(send_act, c) for c in range(1, len(chunks))]

    def send_next(most=1):
        for _ in range(most):
            if later:
                later.pop(0)()

    gossip = []

    def update(here, across):
        grad = lax.dot_general(
            act[:, here], cot[:, across], (((0,), (0,)), ((), ())), preferred_element_type=F32)
        new = w[here, across] - rate[:, across.start:across.start + across.size] * (grad * scale)
        mixed_ref[0, here, across] = new
        give[here, across] = new.astype(BF16)
        at = len(gossip)
        copy = pltpu.make_async_remote_copy(
            src_ref=give.at[here, across], dst_ref=take.at[here, across],
            send_sem=give_sem.at[at], recv_sem=take_sem.at[at],
            device_id=(partner, me), device_id_type=MESH,
        )
        copy.start()
        gossip.append((here, across, copy))

    def project(c):
        here = chunks[c]
        for slot in range(slots):
            term = lax.dot_general(
                act[of(slot), here], wb[here, :], (((1,), (0,)), ((), ())), preferred_element_type=F32)
            part[of(slot), :] = term if c == 0 else part[of(slot), :] + term

    send_cot(0)
    send_act(0)
    send_cot(1)

    load_step.wait()
    step = jnp.full((1, width), step_ref[0], jnp.int32).astype(F32)
    rate = 0.3 / jnp.sqrt(1.0 + step / 50.0)
    load_w.wait()
    load_cot.wait()
    load_act.wait()

    take_cot(0)
    send_next()
    wait_cot(0)
    wait_act(0)
    send_next()
    update(chunks[0], halves[0])
    take_cot(1)
    send_next()
    wb[...] = w[...].astype(BF16)
    wait_cot(1)
    update(chunks[0], halves[1])

    busy = min(2, len(chunks) - 1)
    for c in range(1, len(chunks)):
        wait_act(c)
        send_next()
        update(chunks[c], pl.ds(0, width))
        if c == busy:
            for slot in order + [0]:
                input_grad(slot)
            send_ig(1)
            later += [functools.partial(send_ig, slot) for slot in far]
            for before in range(c):
                project(before)
        if c >= busy:
            project(c)
    send_next(len(later))

    sib_copies = []
    for ahead in list(range(1, chips)) + [0]:
        here = pl.ds(ahead * tokens, tokens)
        to_sib[here, :] = part[of(2 * ahead + 1), :].astype(BF16)
        copy = to_peer(
            to_sib.at[here], from_sib.at[here], sib_send.at[ahead], sib_recv.at[ahead], device(0, 1))
        copy.start()
        sib_copies.append((ahead, copy))
    chip_copies = []
    for ahead, copy in sib_copies:
        here = pl.ds(ahead * tokens, tokens)
        copy.wait_recv()
        if ahead > 0:
            to_chip[here, :] = (part[of(2 * ahead), :] + from_sib[here, :].astype(F32)).astype(BF16)
            on = to_peer(
                to_chip.at[here], from_chip.at[here], chip_send.at[ahead], chip_recv.at[ahead], sender(2 * ahead))
            on.start()
            chip_copies.append((ahead, on))

    for here, across, copy in gossip:
        copy.wait_recv()
        mixed_ref[0, here, across] = 0.5 * (mixed_ref[0, here, across] + take[here, across].astype(F32))

    total = part[of(0), :] + from_sib[pl.ds(0, tokens), :].astype(F32)
    for ahead, on in chip_copies:
        on.wait_recv()
        total = total + from_chip[pl.ds(ahead * tokens, tokens), :].astype(F32)
    proj_ref[0] = (total * scale).astype(BF16)

    for copy in ig_copies.values():
        copy.wait_recv()
    for copy in list(cot_copies.values()) + list(act_copies.values()) + list(ig_copies.values()):
        copy.wait_send()
    for copy in [copy for _, copy in sib_copies + chip_copies] + [copy for _, _, copy in gossip]:
        copy.wait_send()


def pair_kernel(
    bit, half_rows, chunks, scale,
    step_hbm, act_hbm, w_hbm, cot_hbm,
    proj_ref, ig_ref, mixed_ref,
    act, cot, w, ws, acc, p_out, p_in, q, pair_out, pair_in, w_in, s_out, s_in,
    plain_out, plain_in, new_out, new_in, back_out, back_in, step_ref,
    local_sem, ws_send, ws_recv, p_send, p_recv, far_send, far_recv, pair_send, pair_recv,
):
    rep, me = lax.axis_index("rep"), lax.axis_index("fsdp")
    chip, core = me // 2, me % 2
    owners = [me, chip * 2 + 1 - core, (1 - chip) * 2 + core, (1 - chip) * 2 + 1 - core]
    rows, width = w.shape
    size = rows // 4
    sub = half_rows // 2
    plain = pl.ds(2 * half_rows, rows - 2 * half_rows)
    side = (rep // 2 ** bit) % 2
    partner = rep + 2 ** bit - 2 * 2 ** bit * side
    mine, theirs = side * half_rows, (1 - side) * half_rows
    started = []

    def go(src, dst, send, recv, at, device):
        copy = pltpu.make_async_remote_copy(
            src_ref=src, dst_ref=dst, send_sem=send.at[at], recv_sem=recv.at[at],
            device_id=device, device_id_type=MESH,
        )
        copy.start()
        started.append(copy)
        return copy

    core_id, far_id, pair_id = (rep, owners[1]), (rep, owners[2]), (partner, me)

    def part(start, count):
        return pl.ds(pl.multiple_of(start, 16), count)

    def lanes(slot, here):
        return pl.ds(pl.multiple_of(owners[slot] * rows + here.start, 128), here.size)

    def rows_of(slot, here):
        return pl.ds(slot * rows + here.start, here.size)

    head, tail = chunks[0], pl.ds(chunks[0].size, rows - chunks[0].size)
    load_head = pltpu.make_async_copy(w_hbm.at[0, head], w.at[head], local_sem.at[0])
    load_tail = pltpu.make_async_copy(w_hbm.at[0, tail], w.at[tail], local_sem.at[4])
    load_cot = pltpu.make_async_copy(cot_hbm.at[0], cot, local_sem.at[1])
    load_act = pltpu.make_async_copy(act_hbm.at[0], act, local_sem.at[2])
    load_step = pltpu.make_async_copy(step_hbm, step_ref, local_sem.at[3])
    for load in (load_head, load_tail, load_cot, load_act, load_step):
        load.start()

    barrier = pltpu.get_barrier_semaphore()
    for device in (core_id, far_id, pair_id):
        pl.semaphore_signal(barrier, inc=1, device_id=device, device_id_type=MESH)
    load_head.wait()
    ws[head, :] = w[head, :].astype(BF16)
    pl.semaphore_wait(barrier, 3)

    w_copies = {}

    def send_w(slot, k):
        source = 2 if slot == 3 else 0
        w_copies[slot, k] = go(
            ws.at[rows_of(source, chunks[k])], ws.at[rows_of(slot, chunks[k])],
            ws_send, ws_recv, slot * len(chunks) + k, far_id if slot == 2 else core_id)

    def send_w_pair(j):
        return go(
            ws.at[part(theirs + j * sub, sub)], w_in.at[pl.ds(j * sub, sub)],
            pair_send, pair_recv, 7 + j, pair_id)

    send_w(2, 0)
    load_tail.wait()
    ws[tail, :] = w[tail, :].astype(BF16)
    w_pair = [send_w_pair(0)]
    load_cot.wait()
    load_act.wait()

    def term(slot, k):
        return lax.dot_general(
            act[:, lanes(slot, pl.ds(k * size, size))], cot[...],
            (((0,), (0,)), ((), ())), preferred_element_type=F32)

    def send_terms(at, slot):
        copies = []
        for k in range(4):
            here = pl.ds(at * rows + k * size, size)
            p_out[here, :] = term(slot, k).astype(BF16)
            copies.append(go(p_out.at[here], p_in.at[here], p_send, p_recv, at * 4 + k, core_id))
        return copies

    def add_terms(at, slot, copies):
        for k in range(4):
            here = pl.ds(at * rows + k * size, size)
            own = term(slot, k)
            copies[k].wait_recv()
            q[here, :] = own + p_in[here, :].astype(F32)

    pair_copies = {}

    def send_pair(at, j):
        here = pl.ds(at * half_rows + j * sub, sub)
        pair_out[here, :] = q[part(at * rows + theirs + j * sub, sub), :].astype(BF16)
        pair_copies[at, j] = go(
            pair_out.at[here], pair_in.at[here], pair_send, pair_recv, at * 2 + j, pair_id)

    add_terms(1, 2, send_terms(1, 3))
    send_pair(1, 0)
    send_pair(1, 1)
    plain_out[...] = q[pl.ds(rows + 2 * half_rows, rows - 2 * half_rows), :].astype(BF16)
    plain_copy = go(plain_out, plain_in, far_send, far_recv, 0, far_id)
    near = send_terms(0, 1)
    for k in range(len(chunks)):
        send_w(1, k)
    add_terms(0, 0, near)

    load_step.wait()
    step = jnp.full((1, width), step_ref[0], jnp.int32).astype(F32)
    rate = 0.3 / jnp.sqrt(1.0 + step / 50.0) * scale

    def multiply(slot, k):
        block = ws[rows_of(slot, chunks[k]), :]
        across = lanes(slot, chunks[k])
        ig_ref[0, :, across] = (lax.dot_general(
            cot[...], block, (((1,), (1,)), ((), ())), preferred_element_type=F32) * scale).astype(BF16)
        out = jnp.dot(act[:, across], block, preferred_element_type=F32)
        acc[...] = out if (slot, k) == (0, 0) else acc[...] + out

    def arrive(k):
        w_copies[2, k].wait_recv()
        send_w(3, k)

    def forwarded(k):
        w_copies[3, k].wait_recv()
        multiply(3, k)

    last = len(chunks) - 1
    multiply(0, 0)
    far_copies = []
    for j in range(2):
        here = pl.ds(j * sub, sub)
        pair_copies[1, j].wait_recv()
        s_out[here, :] = (
            q[part(rows + mine + j * sub, sub), :] + pair_in[pl.ds(half_rows + j * sub, sub), :].astype(F32)
        ).astype(BF16)
        far_copies.append(go(s_out.at[here], s_in.at[here], far_send, far_recv, 1 + j, far_id))
        send_pair(0, j)
    w_pair.append(send_w_pair(1))
    send_w(2, 1)
    arrive(0)
    for k in range(1, len(chunks)):
        multiply(0, k)
    multiply(2, 0)

    plain_copy.wait_recv()
    send_w(2, 2)
    new = w[plain, :] - rate * (q[plain, :] + plain_in[...].astype(F32))
    mixed_ref[0, plain, :] = new
    new_out[...] = new.astype(BF16)
    new_copy = go(new_out, new_in, pair_send, pair_recv, 4, pair_id)
    for k in range(len(chunks)):
        w_copies[1, k].wait_recv()
        multiply(1, k)
    forwarded(0)

    back_copies = []
    for j in range(2):
        here = pl.ds(j * sub, sub)
        there = part(mine + j * sub, sub)
        w_pair[j].wait_recv()
        pair_copies[0, j].wait_recv()
        far_copies[j].wait_recv()
        if j == 0:
            for k in range(3, len(chunks)):
                send_w(2, k)
        grad = (q[there, :] + pair_in[here, :].astype(F32)) + s_in[here, :].astype(F32)
        mean = 0.5 * ((w[there, :] + w_in[here, :].astype(F32)) - rate * grad)
        mixed_ref[0, there, :] = mean
        back_out[here, :] = mean.astype(BF16)
        back_copies.append(go(back_out.at[here], back_in.at[here], pair_send, pair_recv, 5 + j, pair_id))

    for k in range(1, last):
        arrive(k)
        multiply(2, k)
        if k > 1:
            forwarded(k - 1)
    new_copy.wait_recv()
    mixed_ref[0, plain, :] = 0.5 * (mixed_ref[0, plain, :] + new_in[...].astype(F32))
    arrive(last)
    forwarded(last - 1)
    multiply(2, last)
    for j in range(2):
        back_copies[j].wait_recv()
        mixed_ref[0, part(theirs + j * sub, sub), :] = back_in[pl.ds(j * sub, sub), :].astype(F32)
    forwarded(last)
    proj_ref[0] = (acc[...] * scale).astype(BF16)
    for copy in started:
        copy.wait_send()


def store_kernel(proj_ref, ig_ref, mixed_ref, proj_hbm, ig_hbm, mixed_hbm, sem):
    copies = [pltpu.make_async_copy(proj_ref, proj_hbm, sem.at[0])]
    for src, dst, count in ((ig_ref, ig_hbm, 6), (mixed_ref, mixed_hbm, 8)):
        size = src.shape[1] // count
        for c in range(count):
            here = pl.ds(c * size, size)
            copies.append(pltpu.make_async_copy(src.at[0, here], dst.at[0, here], sem.at[len(copies)]))
    for copy in copies:
        copy.start()
    for copy in copies:
        copy.wait()


def step_kernel(bit, count, activations, weights, cotangent, step_index):
    tokens, features = activations.shape[1:]
    rows, width = weights.shape[1:]
    chips = count // 2
    chunks = [pl.ds(start, 128) for start in range(0, min(rows, 256), 128)]
    chunks += [pl.ds(start, 256) for start in range(256, rows, 256)]
    pieces = len(chunks) + 1
    every = count * tokens
    dma = pltpu.SemaphoreType.DMA
    anywhere = pl.BlockSpec(memory_space=pl.ANY)
    in_vmem = pl.BlockSpec(memory_space=pltpu.VMEM)
    half_rows = rows * 5 // 16
    if chips == 2 and bit < 2 and rows % 1024 == 0:
        part = rows // 8
        blocks = [pl.ds(2 * k * part, 2 * part) for k in range(3)] + [pl.ds(k * part, part) for k in (6, 7)]
        run = functools.partial(pair_kernel, bit, half_rows, blocks, features ** (-0.5))

        def block(count):
            return pltpu.VMEM((count, width), BF16)

        scratch = [
            pltpu.VMEM((tokens, features), BF16), block(tokens),
            pltpu.VMEM((rows, width), F32), block(4 * rows), pltpu.VMEM((tokens, width), F32),
            block(2 * rows), block(2 * rows), pltpu.VMEM((2 * rows, width), F32),
            block(2 * half_rows), block(2 * half_rows), block(half_rows),
            block(half_rows), block(half_rows),
            block(rows - 2 * half_rows), block(rows - 2 * half_rows),
            block(rows - 2 * half_rows), block(rows - 2 * half_rows),
            block(half_rows), block(half_rows), pltpu.SMEM((1,), jnp.int32),
            dma((5,)), dma((4 * len(blocks),)), dma((4 * len(blocks),)), dma((8,)), dma((8,)),
            dma((3,)), dma((3,)), dma((9,)), dma((9,)),
        ]
    else:
        run = functools.partial(kernel, bit, chips, chunks, features ** (-0.5))
        scratch = [
            pltpu.VMEM((every, rows), BF16),
            pltpu.VMEM((every, width), BF16),
            pltpu.VMEM((rows, width), F32),
            pltpu.VMEM((rows, width), BF16),
            pltpu.VMEM((every - tokens, rows), BF16),
            pltpu.VMEM((every, width), F32),
            pltpu.VMEM((chips * tokens, width), BF16),
            pltpu.VMEM((chips * tokens, width), BF16),
            pltpu.VMEM((chips * tokens, width), BF16),
            pltpu.VMEM((chips * tokens, width), BF16),
            pltpu.VMEM((rows, width), BF16),
            pltpu.VMEM((rows, width), BF16),
            pltpu.SMEM((1,), jnp.int32),
            dma((4,)),
            dma((2 * count,)), dma((2 * count,)),
            dma((len(chunks) * count,)), dma((len(chunks) * count,)),
            dma((count,)), dma((count,)),
            dma((chips,)), dma((chips,)),
            dma((chips,)), dma((chips,)),
            dma((pieces,)), dma((pieces,)),
        ]
    results = pl.pallas_call(
        run,
        out_shape=(
            pltpu.VMEM((1, tokens, width), BF16),
            pltpu.VMEM((1, tokens, features), BF16),
            pltpu.VMEM((1, rows, width), F32),
        ),
        in_specs=[anywhere] * 4,
        out_specs=(in_vmem, in_vmem, in_vmem),
        scratch_shapes=scratch,
        compiler_params=pltpu.CompilerParams(
            collective_id=bit, has_side_effects=True, vmem_limit_bytes=40 * 2 ** 20),
        cost_estimate=pl.CostEstimate(
            flops=6 * every * rows * width, bytes_accessed=8 * 2 ** 20, transcendentals=0),
        name="step_bit_%d" % bit,
    )(step_index, activations, weights, cotangent)
    return pl.pallas_call(
        store_kernel,
        out_shape=tuple(jax.ShapeDtypeStruct(part.shape, part.dtype) for part in results),
        in_specs=[anywhere] * 3,
        out_specs=(anywhere, anywhere, anywhere),
        scratch_shapes=[dma((15,))],
        compiler_params=pltpu.CompilerParams(vmem_limit_bytes=2 ** 20),
        name="store",
    )(*results)


def body(count, activations, weights, cotangent, step_index):
    branches = [functools.partial(step_kernel, bit, count) for bit in range(BITS)]
    return lax.switch(step_index[0] % BITS, branches, activations, weights, cotangent, step_index)


def solution(mesh):
    split = P("rep", "fsdp", None)
    return jax.shard_map(
        functools.partial(body, mesh.shape["fsdp"]),
        mesh=mesh,
        in_specs=(split, split, split, P()),
        out_specs=(split, split, split),
        check_vma=False,
    )
```

```python
import functools

import jax
import jax.numpy as jnp
from jax import lax
from jax.experimental import pallas as pl
from jax.experimental.pallas import tpu as pltpu
from jax.sharding import PartitionSpec as P

BITS = 3
MESH = pl.DeviceIdType.MESH
BF16 = jnp.bfloat16
F32 = jnp.float32


def kernel(
    bit, chips, chunks, scale,
    step_hbm, act_hbm, w_hbm, cot_hbm,
    proj_ref, ig_ref, mixed_ref,
    act, cot, w, wb, ig, part, to_sib, from_sib, to_chip, from_chip, give, take, step_ref,
    local_sem, cot_send, cot_recv, act_send, act_recv, ig_send, ig_recv,
    sib_send, sib_recv, chip_send, chip_recv, give_sem, take_sem,
):
    rep, me = lax.axis_index("rep"), lax.axis_index("fsdp")
    chip, core = me // 2, me % 2
    tokens = cot_hbm.shape[1]
    rows = w_hbm.shape[1]
    slots = 2 * chips
    half = 2 ** bit
    partner = rep + half - 2 * half * ((rep // half) % 2)

    def device(ahead, other):
        return ((chip + ahead + chips) % chips) * 2 + (core + other) % 2

    def sender(slot):
        return device(-(slot // 2), slot % 2)

    def receiver(slot):
        return device(slot // 2, slot % 2)

    def to_peer(src, dst, send, recv, peer):
        return pltpu.make_async_remote_copy(
            src_ref=src, dst_ref=dst, send_sem=send, recv_sem=recv,
            device_id=(rep, peer), device_id_type=MESH,
        )

    def of(slot):
        return pl.ds(slot * tokens, tokens)

    def cols(owner):
        return pl.ds(pl.multiple_of(owner * rows, rows), rows)

    def piece(owner, c):
        start, size = chunks[c].start, chunks[c].size
        return pl.ds(pl.multiple_of(owner * rows + start, 128), size)

    load_cot = pltpu.make_async_copy(cot_hbm.at[0], cot.at[of(0)], local_sem.at[0])
    load_act = pltpu.make_async_copy(act_hbm.at[0, :, cols(me)], act.at[of(0)], local_sem.at[1])
    load_w = pltpu.make_async_copy(w_hbm.at[0], w, local_sem.at[2])
    load_step = pltpu.make_async_copy(step_hbm, step_ref, local_sem.at[3])
    load_cot.start()
    load_w.start()
    load_act.start()
    load_step.start()

    barrier = pltpu.get_barrier_semaphore()
    for slot in range(1, slots):
        pl.semaphore_signal(barrier, inc=1, device_id=(rep, receiver(slot)), device_id_type=MESH)
    pl.semaphore_signal(barrier, inc=1, device_id=(partner, me), device_id_type=MESH)
    pl.semaphore_wait(barrier, slots)

    far = list(range(2, slots))
    order = far + [1]
    width = w.shape[1]
    halves = [pl.ds(0, width // 2), pl.ds(width // 2, width // 2)]
    cot_copies, act_copies, ig_copies = {}, {}, {}

    def start_cot(h, src, slot, peer):
        copy = to_peer(
            src, cot.at[of(slot), halves[h]],
            cot_send.at[h * slots + slot], cot_recv.at[h * slots + slot], peer)
        copy.start()
        cot_copies[h, slot] = copy

    def send_cot(h):
        for slot in list(range(2, slots, 2)) + [1]:
            start_cot(h, cot_hbm.at[0, :, halves[h]], slot, receiver(slot))

    def take_cot(h):
        for slot in range(2, slots, 2):
            cot_copies[h, slot].wait_recv()
            start_cot(h, cot.at[of(slot), halves[h]], slot + 1, device(0, 1))

    def wait_cot(h):
        for slot in range(1, slots, 2):
            cot_copies[h, slot].wait_recv()

    def send_act(c):
        for slot in order:
            copy = to_peer(
                act_hbm.at[0, :, piece(receiver(slot), c)],
                act.at[of(slot), chunks[c]],
                act_send.at[c * slots + slot], act_recv.at[c * slots + slot], receiver(slot))
            copy.start()
            act_copies[c, slot] = copy

    def wait_act(c):
        for slot in order:
            act_copies[c, slot].wait_recv()

    def input_grad(slot):
        grad = (lax.dot_general(
            cot[of(slot), :], wb[...], (((1,), (1,)), ((), ())), preferred_element_type=F32
        ) * scale).astype(BF16)
        if slot == 0:
            ig_ref[0, :, cols(me)] = grad
        else:
            ig[of(slot - 1), :] = grad

    def send_ig(slot):
        copy = to_peer(
            ig.at[of(slot - 1)], ig_ref.at[0, :, cols(me)], ig_send.at[slot], ig_recv.at[slot], sender(slot))
        copy.start()
        ig_copies[slot] = copy

    later = [functools.partial(send_act, c) for c in range(1, len(chunks))]

    def send_next(most=1):
        for _ in range(most):
            if later:
                later.pop(0)()

    gossip = []

    def update(here, across):
        grad = lax.dot_general(
            act[:, here], cot[:, across], (((0,), (0,)), ((), ())), preferred_element_type=F32)
        new = w[here, across] - rate[:, across.start:across.start + across.size] * (grad * scale)
        mixed_ref[0, here, across] = new
        give[here, across] = new.astype(BF16)
        at = len(gossip)
        copy = pltpu.make_async_remote_copy(
            src_ref=give.at[here, across], dst_ref=take.at[here, across],
            send_sem=give_sem.at[at], recv_sem=take_sem.at[at],
            device_id=(partner, me), device_id_type=MESH,
        )
        copy.start()
        gossip.append((here, across, copy))

    def project(c):
        here = chunks[c]
        for slot in range(slots):
            term = lax.dot_general(
                act[of(slot), here], wb[here, :], (((1,), (0,)), ((), ())), preferred_element_type=F32)
            part[of(slot), :] = term if c == 0 else part[of(slot), :] + term

    send_cot(0)
    send_act(0)
    send_cot(1)

    load_step.wait()
    step = jnp.full((1, width), step_ref[0], jnp.int32).astype(F32)
    rate = 0.3 / jnp.sqrt(1.0 + step / 50.0)
    load_w.wait()
    load_cot.wait()
    load_act.wait()

    take_cot(0)
    send_next()
    wait_cot(0)
    wait_act(0)
    send_next()
    update(chunks[0], halves[0])
    take_cot(1)
    send_next()
    wb[...] = w[...].astype(BF16)
    wait_cot(1)
    update(chunks[0], halves[1])

    busy = min(2, len(chunks) - 1)
    for c in range(1, len(chunks)):
        wait_act(c)
        send_next()
        update(chunks[c], pl.ds(0, width))
        if c == busy:
            for slot in order + [0]:
                input_grad(slot)
            send_ig(1)
            later += [functools.partial(send_ig, slot) for slot in far]
            for before in range(c):
                project(before)
        if c >= busy:
            project(c)
    send_next(len(later))

    sib_copies = []
    for ahead in list(range(1, chips)) + [0]:
        here = pl.ds(ahead * tokens, tokens)
        to_sib[here, :] = part[of(2 * ahead + 1), :].astype(BF16)
        copy = to_peer(
            to_sib.at[here], from_sib.at[here], sib_send.at[ahead], sib_recv.at[ahead], device(0, 1))
        copy.start()
        sib_copies.append((ahead, copy))
    chip_copies = []
    for ahead, copy in sib_copies:
        here = pl.ds(ahead * tokens, tokens)
        copy.wait_recv()
        if ahead > 0:
            to_chip[here, :] = (part[of(2 * ahead), :] + from_sib[here, :].astype(F32)).astype(BF16)
            on = to_peer(
                to_chip.at[here], from_chip.at[here], chip_send.at[ahead], chip_recv.at[ahead], sender(2 * ahead))
            on.start()
            chip_copies.append((ahead, on))

    for here, across, copy in gossip:
        copy.wait_recv()
        mixed_ref[0, here, across] = 0.5 * (mixed_ref[0, here, across] + take[here, across].astype(F32))

    total = part[of(0), :] + from_sib[pl.ds(0, tokens), :].astype(F32)
    for ahead, on in chip_copies:
        on.wait_recv()
        total = total + from_chip[pl.ds(ahead * tokens, tokens), :].astype(F32)
    proj_ref[0] = (total * scale).astype(BF16)

    for copy in ig_copies.values():
        copy.wait_recv()
    for copy in list(cot_copies.values()) + list(act_copies.values()) + list(ig_copies.values()):
        copy.wait_send()
    for copy in [copy for _, copy in sib_copies + chip_copies] + [copy for _, _, copy in gossip]:
        copy.wait_send()


def pair_kernel(
    bit, half_rows, chunks, scale,
    step_hbm, act_hbm, w_hbm, cot_hbm,
    proj_ref, ig_ref, mixed_ref,
    act, cot, w, ws, acc, p_out, p_in, q, pair_out, pair_in, w_in, s_out, s_in,
    plain_out, plain_in, new_out, new_in, back_out, back_in, step_ref,
    local_sem, ws_send, ws_recv, p_send, p_recv, far_send, far_recv, pair_send, pair_recv,
):
    rep, me = lax.axis_index("rep"), lax.axis_index("fsdp")
    chip, core = me // 2, me % 2
    owners = [me, chip * 2 + 1 - core, (1 - chip) * 2 + core, (1 - chip) * 2 + 1 - core]
    rows, width = w.shape
    size = rows // 4
    sub = half_rows // 2
    plain = pl.ds(2 * half_rows, rows - 2 * half_rows)
    side = (rep // 2 ** bit) % 2
    partner = rep + 2 ** bit - 2 * 2 ** bit * side
    mine, theirs = side * half_rows, (1 - side) * half_rows
    started = []

    def go(src, dst, send, recv, at, device):
        copy = pltpu.make_async_remote_copy(
            src_ref=src, dst_ref=dst, send_sem=send.at[at], recv_sem=recv.at[at],
            device_id=device, device_id_type=MESH,
        )
        copy.start()
        started.append(copy)
        return copy

    core_id, far_id, pair_id = (rep, owners[1]), (rep, owners[2]), (partner, me)

    def part(start, count):
        return pl.ds(pl.multiple_of(start, 16), count)

    def lanes(slot, here):
        return pl.ds(pl.multiple_of(owners[slot] * rows + here.start, 128), here.size)

    def rows_of(slot, here):
        return pl.ds(slot * rows + here.start, here.size)

    head, tail = chunks[0], pl.ds(chunks[0].size, rows - chunks[0].size)
    load_head = pltpu.make_async_copy(w_hbm.at[0, head], w.at[head], local_sem.at[0])
    load_tail = pltpu.make_async_copy(w_hbm.at[0, tail], w.at[tail], local_sem.at[4])
    load_cot = pltpu.make_async_copy(cot_hbm.at[0], cot, local_sem.at[1])
    load_act = pltpu.make_async_copy(act_hbm.at[0], act, local_sem.at[2])
    load_step = pltpu.make_async_copy(step_hbm, step_ref, local_sem.at[3])
    for load in (load_head, load_tail, load_cot, load_act, load_step):
        load.start()

    barrier = pltpu.get_barrier_semaphore()
    for device in (core_id, far_id, pair_id):
        pl.semaphore_signal(barrier, inc=1, device_id=device, device_id_type=MESH)
    load_head.wait()
    ws[head, :] = w[head, :].astype(BF16)
    pl.semaphore_wait(barrier, 3)

    w_copies = {}

    def send_w(slot, k):
        source = 2 if slot == 3 else 0
        w_copies[slot, k] = go(
            ws.at[rows_of(source, chunks[k])], ws.at[rows_of(slot, chunks[k])],
            ws_send, ws_recv, slot * len(chunks) + k, far_id if slot == 2 else core_id)

    def send_w_pair(j):
        return go(
            ws.at[part(theirs + j * sub, sub)], w_in.at[pl.ds(j * sub, sub)],
            pair_send, pair_recv, 7 + j, pair_id)

    send_w(2, 0)
    load_tail.wait()
    ws[tail, :] = w[tail, :].astype(BF16)
    w_pair = [send_w_pair(0)]
    load_cot.wait()
    load_act.wait()

    def term(slot, k):
        return lax.dot_general(
            act[:, lanes(slot, pl.ds(k * size, size))], cot[...],
            (((0,), (0,)), ((), ())), preferred_element_type=F32)

    def send_terms(at, slot):
        copies = []
        for k in range(4):
            here = pl.ds(at * rows + k * size, size)
            p_out[here, :] = term(slot, k).astype(BF16)
            copies.append(go(p_out.at[here], p_in.at[here], p_send, p_recv, at * 4 + k, core_id))
        return copies

    def add_terms(at, slot, copies):
        for k in range(4):
            here = pl.ds(at * rows + k * size, size)
            own = term(slot, k)
            copies[k].wait_recv()
            q[here, :] = own + p_in[here, :].astype(F32)

    pair_copies = {}

    def send_pair(at, j):
        here = pl.ds(at * half_rows + j * sub, sub)
        pair_out[here, :] = q[part(at * rows + theirs + j * sub, sub), :].astype(BF16)
        pair_copies[at, j] = go(
            pair_out.at[here], pair_in.at[here], pair_send, pair_recv, at * 2 + j, pair_id)

    add_terms(1, 2, send_terms(1, 3))
    send_pair(1, 0)
    send_pair(1, 1)
    plain_out[...] = q[pl.ds(rows + 2 * half_rows, rows - 2 * half_rows), :].astype(BF16)
    plain_copy = go(plain_out, plain_in, far_send, far_recv, 0, far_id)
    near = send_terms(0, 1)
    for k in range(len(chunks)):
        send_w(1, k)
    add_terms(0, 0, near)

    load_step.wait()
    step = jnp.full((1, width), step_ref[0], jnp.int32).astype(F32)
    rate = 0.3 / jnp.sqrt(1.0 + step / 50.0) * scale

    def multiply(slot, k):
        block = ws[rows_of(slot, chunks[k]), :]
        across = lanes(slot, chunks[k])
        ig_ref[0, :, across] = (lax.dot_general(
            cot[...], block, (((1,), (1,)), ((), ())), preferred_element_type=F32) * scale).astype(BF16)
        out = jnp.dot(act[:, across], block, preferred_element_type=F32)
        acc[...] = out if (slot, k) == (0, 0) else acc[...] + out

    def arrive(k):
        w_copies[2, k].wait_recv()
        send_w(3, k)

    def forwarded(k):
        w_copies[3, k].wait_recv()
        multiply(3, k)

    last = len(chunks) - 1
    multiply(0, 0)
    far_copies = []
    for j in range(2):
        here = pl.ds(j * sub, sub)
        pair_copies[1, j].wait_recv()
        s_out[here, :] = (
            q[part(rows + mine + j * sub, sub), :] + pair_in[pl.ds(half_rows + j * sub, sub), :].astype(F32)
        ).astype(BF16)
        far_copies.append(go(s_out.at[here], s_in.at[here], far_send, far_recv, 1 + j, far_id))
        send_pair(0, j)
    w_pair.append(send_w_pair(1))
    send_w(2, 1)
    arrive(0)
    for k in range(1, len(chunks)):
        multiply(0, k)
    multiply(2, 0)

    plain_copy.wait_recv()
    send_w(2, 2)
    new = w[plain, :] - rate * (q[plain, :] + plain_in[...].astype(F32))
    mixed_ref[0, plain, :] = new
    new_out[...] = new.astype(BF16)
    new_copy = go(new_out, new_in, pair_send, pair_recv, 4, pair_id)
    for k in range(len(chunks)):
        w_copies[1, k].wait_recv()
        multiply(1, k)
    forwarded(0)

    back_copies = []
    for j in range(2):
        here = pl.ds(j * sub, sub)
        there = part(mine + j * sub, sub)
        w_pair[j].wait_recv()
        pair_copies[0, j].wait_recv()
        far_copies[j].wait_recv()
        if j == 0:
            for k in range(3, len(chunks)):
                send_w(2, k)
        grad = (q[there, :] + pair_in[here, :].astype(F32)) + s_in[here, :].astype(F32)
        mean = 0.5 * ((w[there, :] + w_in[here, :].astype(F32)) - rate * grad)
        mixed_ref[0, there, :] = mean
        back_out[here, :] = mean.astype(BF16)
        back_copies.append(go(back_out.at[here], back_in.at[here], pair_send, pair_recv, 5 + j, pair_id))

    for k in range(1, last):
        arrive(k)
        multiply(2, k)
        if k > 1:
            forwarded(k - 1)
    new_copy.wait_recv()
    mixed_ref[0, plain, :] = 0.5 * (mixed_ref[0, plain, :] + new_in[...].astype(F32))
    arrive(last)
    forwarded(last - 1)
    multiply(2, last)
    for j in range(2):
        back_copies[j].wait_recv()
        mixed_ref[0, part(theirs + j * sub, sub), :] = back_in[pl.ds(j * sub, sub), :].astype(F32)
    forwarded(last)
    proj_ref[0] = (acc[...] * scale).astype(BF16)
    for copy in started:
        copy.wait_send()


def store_kernel(proj_ref, ig_ref, mixed_ref, proj_hbm, ig_hbm, mixed_hbm, sem):
    copies = [pltpu.make_async_copy(proj_ref, proj_hbm, sem.at[0])]
    for src, dst, count in ((ig_ref, ig_hbm, 4), (mixed_ref, mixed_hbm, 4)):
        size = src.shape[1] // count
        for c in range(count):
            here = pl.ds(c * size, size)
            copies.append(pltpu.make_async_copy(src.at[0, here], dst.at[0, here], sem.at[len(copies)]))
    for copy in copies:
        copy.start()
    for copy in copies:
        copy.wait()


def step_kernel(bit, count, activations, weights, cotangent, step_index):
    tokens, features = activations.shape[1:]
    rows, width = weights.shape[1:]
    chips = count // 2
    chunks = [pl.ds(start, 128) for start in range(0, min(rows, 256), 128)]
    chunks += [pl.ds(start, 256) for start in range(256, rows, 256)]
    pieces = len(chunks) + 1
    every = count * tokens
    dma = pltpu.SemaphoreType.DMA
    anywhere = pl.BlockSpec(memory_space=pl.ANY)
    in_vmem = pl.BlockSpec(memory_space=pltpu.VMEM)
    half_rows = rows * 11 // 32
    if chips == 2 and bit < 2 and rows % 1024 == 0:
        part = rows // 8
        blocks = [pl.ds(2 * k * part, 2 * part) for k in range(3)] + [pl.ds(k * part, part) for k in (6, 7)]
        run = functools.partial(pair_kernel, bit, half_rows, blocks, features ** (-0.5))

        def block(count):
            return pltpu.VMEM((count, width), BF16)

        scratch = [
            pltpu.VMEM((tokens, features), BF16), block(tokens),
            pltpu.VMEM((rows, width), F32), block(4 * rows), pltpu.VMEM((tokens, width), F32),
            block(2 * rows), block(2 * rows), pltpu.VMEM((2 * rows, width), F32),
            block(2 * half_rows), block(2 * half_rows), block(half_rows),
            block(half_rows), block(half_rows),
            block(rows - 2 * half_rows), block(rows - 2 * half_rows),
            block(rows - 2 * half_rows), block(rows - 2 * half_rows),
            block(half_rows), block(half_rows), pltpu.SMEM((1,), jnp.int32),
            dma((5,)), dma((4 * len(blocks),)), dma((4 * len(blocks),)), dma((8,)), dma((8,)),
            dma((3,)), dma((3,)), dma((9,)), dma((9,)),
        ]
    else:
        run = functools.partial(kernel, bit, chips, chunks, features ** (-0.5))
        scratch = [
            pltpu.VMEM((every, rows), BF16),
            pltpu.VMEM((every, width), BF16),
            pltpu.VMEM((rows, width), F32),
            pltpu.VMEM((rows, width), BF16),
            pltpu.VMEM((every - tokens, rows), BF16),
            pltpu.VMEM((every, width), F32),
            pltpu.VMEM((chips * tokens, width), BF16),
            pltpu.VMEM((chips * tokens, width), BF16),
            pltpu.VMEM((chips * tokens, width), BF16),
            pltpu.VMEM((chips * tokens, width), BF16),
            pltpu.VMEM((rows, width), BF16),
            pltpu.VMEM((rows, width), BF16),
            pltpu.SMEM((1,), jnp.int32),
            dma((4,)),
            dma((2 * count,)), dma((2 * count,)),
            dma((len(chunks) * count,)), dma((len(chunks) * count,)),
            dma((count,)), dma((count,)),
            dma((chips,)), dma((chips,)),
            dma((chips,)), dma((chips,)),
            dma((pieces,)), dma((pieces,)),
        ]
    results = pl.pallas_call(
        run,
        out_shape=(
            pltpu.VMEM((1, tokens, width), BF16),
            pltpu.VMEM((1, tokens, features), BF16),
            pltpu.VMEM((1, rows, width), F32),
        ),
        in_specs=[anywhere] * 4,
        out_specs=(in_vmem, in_vmem, in_vmem),
        scratch_shapes=scratch,
        compiler_params=pltpu.CompilerParams(
            collective_id=bit, has_side_effects=True, vmem_limit_bytes=40 * 2 ** 20),
        cost_estimate=pl.CostEstimate(
            flops=6 * every * rows * width, bytes_accessed=8 * 2 ** 20, transcendentals=0),
        name="step_bit_%d" % bit,
    )(step_index, activations, weights, cotangent)
    return pl.pallas_call(
        store_kernel,
        out_shape=tuple(jax.ShapeDtypeStruct(part.shape, part.dtype) for part in results),
        in_specs=[anywhere] * 3,
        out_specs=(anywhere, anywhere, anywhere),
        scratch_shapes=[dma((9,))],
        compiler_params=pltpu.CompilerParams(vmem_limit_bytes=2 ** 20),
        name="store",
    )(*results)


def body(count, activations, weights, cotangent, step_index):
    branches = [functools.partial(step_kernel, bit, count) for bit in range(BITS)]
    return lax.switch(step_index[0] % BITS, branches, activations, weights, cotangent, step_index)


def solution(mesh):
    split = P("rep", "fsdp", None)
    return jax.shard_map(
        functools.partial(body, mesh.shape["fsdp"]),
        mesh=mesh,
        in_specs=(split, split, split, P()),
        out_specs=(split, split, split),
        check_vma=False,
    )
```

```python
import functools

import jax
import jax.numpy as jnp
from jax import lax
from jax.experimental import pallas as pl
from jax.experimental.pallas import tpu as pltpu
from jax.sharding import PartitionSpec as P

BITS = 3
MESH = pl.DeviceIdType.MESH
BF16 = jnp.bfloat16
F32 = jnp.float32


def kernel(
    bit, chips, chunks, scale,
    step_hbm, act_hbm, w_hbm, cot_hbm,
    proj_ref, ig_ref, mixed_ref,
    act, cot, w, wb, ig, part, to_sib, from_sib, to_chip, from_chip, give, take, step_ref,
    local_sem, cot_send, cot_recv, act_send, act_recv, ig_send, ig_recv,
    sib_send, sib_recv, chip_send, chip_recv, give_sem, take_sem,
):
    rep, me = lax.axis_index("rep"), lax.axis_index("fsdp")
    chip, core = me // 2, me % 2
    tokens = cot_hbm.shape[1]
    rows = w_hbm.shape[1]
    slots = 2 * chips
    half = 2 ** bit
    partner = rep + half - 2 * half * ((rep // half) % 2)

    def device(ahead, other):
        return ((chip + ahead + chips) % chips) * 2 + (core + other) % 2

    def sender(slot):
        return device(-(slot // 2), slot % 2)

    def receiver(slot):
        return device(slot // 2, slot % 2)

    def to_peer(src, dst, send, recv, peer):
        return pltpu.make_async_remote_copy(
            src_ref=src, dst_ref=dst, send_sem=send, recv_sem=recv,
            device_id=(rep, peer), device_id_type=MESH,
        )

    def of(slot):
        return pl.ds(slot * tokens, tokens)

    def cols(owner):
        return pl.ds(pl.multiple_of(owner * rows, rows), rows)

    def piece(owner, c):
        start, size = chunks[c].start, chunks[c].size
        return pl.ds(pl.multiple_of(owner * rows + start, 128), size)

    load_cot = pltpu.make_async_copy(cot_hbm.at[0], cot.at[of(0)], local_sem.at[0])
    load_act = pltpu.make_async_copy(act_hbm.at[0, :, cols(me)], act.at[of(0)], local_sem.at[1])
    load_w = pltpu.make_async_copy(w_hbm.at[0], w, local_sem.at[2])
    load_step = pltpu.make_async_copy(step_hbm, step_ref, local_sem.at[3])
    load_cot.start()
    load_w.start()
    load_act.start()
    load_step.start()

    barrier = pltpu.get_barrier_semaphore()
    for slot in range(1, slots):
        pl.semaphore_signal(barrier, inc=1, device_id=(rep, receiver(slot)), device_id_type=MESH)
    pl.semaphore_signal(barrier, inc=1, device_id=(partner, me), device_id_type=MESH)
    pl.semaphore_wait(barrier, slots)

    far = list(range(2, slots))
    order = far + [1]
    width = w.shape[1]
    spans = [pl.ds(0, width // 4), pl.ds(width // 4, width // 4), pl.ds(width // 2, width // 2)]
    cot_copies, act_copies, ig_copies = {}, {}, {}

    def start_cot(h, src, slot, peer):
        copy = to_peer(
            src, cot.at[of(slot), spans[h]],
            cot_send.at[h * slots + slot], cot_recv.at[h * slots + slot], peer)
        copy.start()
        cot_copies[h, slot] = copy

    def send_cot(h):
        for slot in list(range(2, slots, 2)) + [1]:
            start_cot(h, cot_hbm.at[0, :, spans[h]], slot, receiver(slot))

    def take_cot(h):
        for slot in range(2, slots, 2):
            cot_copies[h, slot].wait_recv()
            start_cot(h, cot.at[of(slot), spans[h]], slot + 1, device(0, 1))

    def wait_cot(h):
        for slot in range(1, slots, 2):
            cot_copies[h, slot].wait_recv()

    def send_act(c):
        for slot in order:
            copy = to_peer(
                act_hbm.at[0, :, piece(receiver(slot), c)],
                act.at[of(slot), chunks[c]],
                act_send.at[c * slots + slot], act_recv.at[c * slots + slot], receiver(slot))
            copy.start()
            act_copies[c, slot] = copy

    def wait_act(c):
        for slot in order:
            act_copies[c, slot].wait_recv()

    def input_grad(slot):
        grad = (lax.dot_general(
            cot[of(slot), :], wb[...], (((1,), (1,)), ((), ())), preferred_element_type=F32
        ) * scale).astype(BF16)
        if slot == 0:
            ig_ref[0, :, cols(me)] = grad
        else:
            ig[of(slot - 1), :] = grad

    def send_ig(slot):
        copy = to_peer(
            ig.at[of(slot - 1)], ig_ref.at[0, :, cols(me)], ig_send.at[slot], ig_recv.at[slot], sender(slot))
        copy.start()
        ig_copies[slot] = copy

    later = [functools.partial(send_act, c) for c in range(1, len(chunks))]

    def send_next(most=1):
        for _ in range(most):
            if later:
                later.pop(0)()

    gossip = []

    def update(here, across):
        grad = lax.dot_general(
            act[:, here], cot[:, across], (((0,), (0,)), ((), ())), preferred_element_type=F32)
        new = w[here, across] - rate[:, across.start:across.start + across.size] * (grad * scale)
        mixed_ref[0, here, across] = new
        give[here, across] = new.astype(BF16)
        at = len(gossip)
        copy = pltpu.make_async_remote_copy(
            src_ref=give.at[here, across], dst_ref=take.at[here, across],
            send_sem=give_sem.at[at], recv_sem=take_sem.at[at],
            device_id=(partner, me), device_id_type=MESH,
        )
        copy.start()
        gossip.append((here, across, copy))

    def project(c):
        here = chunks[c]
        for slot in range(slots):
            term = lax.dot_general(
                act[of(slot), here], wb[here, :], (((1,), (0,)), ((), ())), preferred_element_type=F32)
            part[of(slot), :] = term if c == 0 else part[of(slot), :] + term

    send_cot(0)
    send_act(0)
    send_cot(1)
    send_cot(2)

    load_step.wait()
    step = jnp.full((1, width), step_ref[0], jnp.int32).astype(F32)
    rate = 0.3 / jnp.sqrt(1.0 + step / 50.0)
    load_w.wait()
    load_cot.wait()
    load_act.wait()

    take_cot(0)
    send_next()
    wait_cot(0)
    wait_act(0)
    send_next()
    update(chunks[0], spans[0])
    take_cot(1)
    wait_cot(1)
    update(chunks[0], spans[1])
    take_cot(2)
    send_next()
    wb[...] = w[...].astype(BF16)
    wait_cot(2)
    update(chunks[0], spans[2])

    busy = min(2, len(chunks) - 1)
    for c in range(1, len(chunks)):
        wait_act(c)
        send_next()
        update(chunks[c], pl.ds(0, width))
        if c == busy:
            for slot in order + [0]:
                input_grad(slot)
            send_ig(1)
            later += [functools.partial(send_ig, slot) for slot in far]
            for before in range(c):
                project(before)
        if c >= busy:
            project(c)
    send_next(len(later))

    sib_copies = []
    for ahead in list(range(1, chips)) + [0]:
        here = pl.ds(ahead * tokens, tokens)
        to_sib[here, :] = part[of(2 * ahead + 1), :].astype(BF16)
        copy = to_peer(
            to_sib.at[here], from_sib.at[here], sib_send.at[ahead], sib_recv.at[ahead], device(0, 1))
        copy.start()
        sib_copies.append((ahead, copy))
    chip_copies = []
    for ahead, copy in sib_copies:
        here = pl.ds(ahead * tokens, tokens)
        copy.wait_recv()
        if ahead > 0:
            to_chip[here, :] = (part[of(2 * ahead), :] + from_sib[here, :].astype(F32)).astype(BF16)
            on = to_peer(
                to_chip.at[here], from_chip.at[here], chip_send.at[ahead], chip_recv.at[ahead], sender(2 * ahead))
            on.start()
            chip_copies.append((ahead, on))

    for here, across, copy in gossip:
        copy.wait_recv()
        mixed_ref[0, here, across] = 0.5 * (mixed_ref[0, here, across] + take[here, across].astype(F32))

    total = part[of(0), :] + from_sib[pl.ds(0, tokens), :].astype(F32)
    for ahead, on in chip_copies:
        on.wait_recv()
        total = total + from_chip[pl.ds(ahead * tokens, tokens), :].astype(F32)
    proj_ref[0] = (total * scale).astype(BF16)

    for copy in ig_copies.values():
        copy.wait_recv()
    for copy in list(cot_copies.values()) + list(act_copies.values()) + list(ig_copies.values()):
        copy.wait_send()
    for copy in [copy for _, copy in sib_copies + chip_copies] + [copy for _, _, copy in gossip]:
        copy.wait_send()


def pair_kernel(
    bit, half_rows, chunks, scale,
    step_hbm, act_hbm, w_hbm, cot_hbm,
    proj_ref, ig_ref, mixed_ref,
    act, cot, w, ws, acc, p_out, p_in, q, pair_out, pair_in, w_in, s_out, s_in,
    plain_out, plain_in, new_out, new_in, back_out, back_in, step_ref,
    local_sem, ws_send, ws_recv, p_send, p_recv, far_send, far_recv, pair_send, pair_recv,
):
    rep, me = lax.axis_index("rep"), lax.axis_index("fsdp")
    chip, core = me // 2, me % 2
    owners = [me, chip * 2 + 1 - core, (1 - chip) * 2 + core, (1 - chip) * 2 + 1 - core]
    rows, width = w.shape
    size = rows // 4
    sub = half_rows // 2
    plain = pl.ds(2 * half_rows, rows - 2 * half_rows)
    side = (rep // 2 ** bit) % 2
    partner = rep + 2 ** bit - 2 * 2 ** bit * side
    mine, theirs = side * half_rows, (1 - side) * half_rows
    started = []

    def go(src, dst, send, recv, at, device):
        copy = pltpu.make_async_remote_copy(
            src_ref=src, dst_ref=dst, send_sem=send.at[at], recv_sem=recv.at[at],
            device_id=device, device_id_type=MESH,
        )
        copy.start()
        started.append(copy)
        return copy

    core_id, far_id, pair_id = (rep, owners[1]), (rep, owners[2]), (partner, me)

    def part(start, count):
        return pl.ds(pl.multiple_of(start, 16), count)

    def lanes(slot, here):
        return pl.ds(pl.multiple_of(owners[slot] * rows + here.start, 128), here.size)

    def rows_of(slot, here):
        return pl.ds(slot * rows + here.start, here.size)

    head, tail = chunks[0], pl.ds(chunks[0].size, rows - chunks[0].size)
    load_head = pltpu.make_async_copy(w_hbm.at[0, head], w.at[head], local_sem.at[0])
    load_tail = pltpu.make_async_copy(w_hbm.at[0, tail], w.at[tail], local_sem.at[4])
    load_cot = pltpu.make_async_copy(cot_hbm.at[0], cot, local_sem.at[1])
    load_act = pltpu.make_async_copy(act_hbm.at[0], act, local_sem.at[2])
    load_step = pltpu.make_async_copy(step_hbm, step_ref, local_sem.at[3])
    for load in (load_head, load_tail, load_cot, load_act, load_step):
        load.start()

    barrier = pltpu.get_barrier_semaphore()
    for device in (core_id, far_id, pair_id):
        pl.semaphore_signal(barrier, inc=1, device_id=device, device_id_type=MESH)
    load_head.wait()
    ws[head, :] = w[head, :].astype(BF16)
    pl.semaphore_wait(barrier, 3)

    w_copies = {}

    def send_w(slot, k):
        source = 2 if slot == 3 else 0
        w_copies[slot, k] = go(
            ws.at[rows_of(source, chunks[k])], ws.at[rows_of(slot, chunks[k])],
            ws_send, ws_recv, slot * len(chunks) + k, far_id if slot == 2 else core_id)

    def send_w_pair(j):
        return go(
            ws.at[part(theirs + j * sub, sub)], w_in.at[pl.ds(j * sub, sub)],
            pair_send, pair_recv, 7 + j, pair_id)

    send_w(2, 0)
    load_tail.wait()
    ws[tail, :] = w[tail, :].astype(BF16)
    w_pair = [send_w_pair(0)]
    load_cot.wait()
    load_act.wait()

    def term(slot, k):
        return lax.dot_general(
            act[:, lanes(slot, pl.ds(k * size, size))], cot[...],
            (((0,), (0,)), ((), ())), preferred_element_type=F32)

    def send_terms(at, slot):
        copies = []
        for k in range(4):
            here = pl.ds(at * rows + k * size, size)
            p_out[here, :] = term(slot, k).astype(BF16)
            copies.append(go(p_out.at[here], p_in.at[here], p_send, p_recv, at * 4 + k, core_id))
        return copies

    def add_terms(at, slot, copies):
        for k in range(4):
            here = pl.ds(at * rows + k * size, size)
            own = term(slot, k)
            copies[k].wait_recv()
            q[here, :] = own + p_in[here, :].astype(F32)

    pair_copies = {}

    def send_pair(at, j):
        here = pl.ds(at * half_rows + j * sub, sub)
        pair_out[here, :] = q[part(at * rows + theirs + j * sub, sub), :].astype(BF16)
        pair_copies[at, j] = go(
            pair_out.at[here], pair_in.at[here], pair_send, pair_recv, at * 2 + j, pair_id)

    add_terms(1, 2, send_terms(1, 3))
    send_pair(1, 0)
    send_pair(1, 1)
    plain_out[...] = q[pl.ds(rows + 2 * half_rows, rows - 2 * half_rows), :].astype(BF16)
    plain_copy = go(plain_out, plain_in, far_send, far_recv, 0, far_id)
    near = send_terms(0, 1)
    for k in range(len(chunks)):
        send_w(1, k)
    add_terms(0, 0, near)

    load_step.wait()
    step = jnp.full((1, width), step_ref[0], jnp.int32).astype(F32)
    rate = 0.3 / jnp.sqrt(1.0 + step / 50.0) * scale

    def multiply(slot, k):
        block = ws[rows_of(slot, chunks[k]), :]
        across = lanes(slot, chunks[k])
        ig_ref[0, :, across] = (lax.dot_general(
            cot[...], block, (((1,), (1,)), ((), ())), preferred_element_type=F32) * scale).astype(BF16)
        out = jnp.dot(act[:, across], block, preferred_element_type=F32)
        acc[...] = out if (slot, k) == (0, 0) else acc[...] + out

    def arrive(k):
        w_copies[2, k].wait_recv()
        send_w(3, k)

    def forwarded(k):
        w_copies[3, k].wait_recv()
        multiply(3, k)

    last = len(chunks) - 1
    multiply(0, 0)
    far_copies = []
    for j in range(2):
        here = pl.ds(j * sub, sub)
        pair_copies[1, j].wait_recv()
        s_out[here, :] = (
            q[part(rows + mine + j * sub, sub), :] + pair_in[pl.ds(half_rows + j * sub, sub), :].astype(F32)
        ).astype(BF16)
        far_copies.append(go(s_out.at[here], s_in.at[here], far_send, far_recv, 1 + j, far_id))
        send_pair(0, j)
    w_pair.append(send_w_pair(1))
    send_w(2, 1)
    arrive(0)
    for k in range(1, len(chunks)):
        multiply(0, k)
    multiply(2, 0)

    plain_copy.wait_recv()
    send_w(2, 2)
    new = w[plain, :] - rate * (q[plain, :] + plain_in[...].astype(F32))
    mixed_ref[0, plain, :] = new
    new_out[...] = new.astype(BF16)
    new_copy = go(new_out, new_in, pair_send, pair_recv, 4, pair_id)
    for k in range(len(chunks)):
        w_copies[1, k].wait_recv()
        multiply(1, k)
    forwarded(0)

    back_copies = []
    for j in range(2):
        here = pl.ds(j * sub, sub)
        there = part(mine + j * sub, sub)
        w_pair[j].wait_recv()
        pair_copies[0, j].wait_recv()
        far_copies[j].wait_recv()
        if j == 0:
            for k in range(3, len(chunks)):
                send_w(2, k)
        grad = (q[there, :] + pair_in[here, :].astype(F32)) + s_in[here, :].astype(F32)
        mean = 0.5 * ((w[there, :] + w_in[here, :].astype(F32)) - rate * grad)
        mixed_ref[0, there, :] = mean
        back_out[here, :] = mean.astype(BF16)
        back_copies.append(go(back_out.at[here], back_in.at[here], pair_send, pair_recv, 5 + j, pair_id))

    for k in range(1, last):
        arrive(k)
        multiply(2, k)
        if k > 1:
            forwarded(k - 1)
    new_copy.wait_recv()
    mixed_ref[0, plain, :] = 0.5 * (mixed_ref[0, plain, :] + new_in[...].astype(F32))
    arrive(last)
    forwarded(last - 1)
    multiply(2, last)
    for j in range(2):
        back_copies[j].wait_recv()
        mixed_ref[0, part(theirs + j * sub, sub), :] = back_in[pl.ds(j * sub, sub), :].astype(F32)
    forwarded(last)
    proj_ref[0] = (acc[...] * scale).astype(BF16)
    for copy in started:
        copy.wait_send()


def store_kernel(proj_ref, ig_ref, mixed_ref, proj_hbm, ig_hbm, mixed_hbm, sem):
    copies = [pltpu.make_async_copy(proj_ref, proj_hbm, sem.at[0])]
    for src, dst, count in ((ig_ref, ig_hbm, 4), (mixed_ref, mixed_hbm, 4)):
        size = src.shape[1] // count
        for c in range(count):
            here = pl.ds(c * size, size)
            copies.append(pltpu.make_async_copy(src.at[0, here], dst.at[0, here], sem.at[len(copies)]))
    for copy in copies:
        copy.start()
    for copy in copies:
        copy.wait()


def step_kernel(bit, count, activations, weights, cotangent, step_index):
    tokens, features = activations.shape[1:]
    rows, width = weights.shape[1:]
    chips = count // 2
    chunks = [pl.ds(start, 128) for start in range(0, min(rows, 256), 128)]
    chunks += [pl.ds(start, 256) for start in range(256, rows, 256)]
    pieces = len(chunks) + 2
    every = count * tokens
    dma = pltpu.SemaphoreType.DMA
    anywhere = pl.BlockSpec(memory_space=pl.ANY)
    in_vmem = pl.BlockSpec(memory_space=pltpu.VMEM)
    half_rows = rows * 11 // 32
    if chips == 2 and bit < 2 and rows % 1024 == 0:
        part = rows // 8
        blocks = [pl.ds(2 * k * part, 2 * part) for k in range(3)] + [pl.ds(k * part, part) for k in (6, 7)]
        run = functools.partial(pair_kernel, bit, half_rows, blocks, features ** (-0.5))

        def block(count):
            return pltpu.VMEM((count, width), BF16)

        scratch = [
            pltpu.VMEM((tokens, features), BF16), block(tokens),
            pltpu.VMEM((rows, width), F32), block(4 * rows), pltpu.VMEM((tokens, width), F32),
            block(2 * rows), block(2 * rows), pltpu.VMEM((2 * rows, width), F32),
            block(2 * half_rows), block(2 * half_rows), block(half_rows),
            block(half_rows), block(half_rows),
            block(rows - 2 * half_rows), block(rows - 2 * half_rows),
            block(rows - 2 * half_rows), block(rows - 2 * half_rows),
            block(half_rows), block(half_rows), pltpu.SMEM((1,), jnp.int32),
            dma((5,)), dma((4 * len(blocks),)), dma((4 * len(blocks),)), dma((8,)), dma((8,)),
            dma((3,)), dma((3,)), dma((9,)), dma((9,)),
        ]
    else:
        run = functools.partial(kernel, bit, chips, chunks, features ** (-0.5))
        scratch = [
            pltpu.VMEM((every, rows), BF16),
            pltpu.VMEM((every, width), BF16),
            pltpu.VMEM((rows, width), F32),
            pltpu.VMEM((rows, width), BF16),
            pltpu.VMEM((every - tokens, rows), BF16),
            pltpu.VMEM((every, width), F32),
            pltpu.VMEM((chips * tokens, width), BF16),
            pltpu.VMEM((chips * tokens, width), BF16),
            pltpu.VMEM((chips * tokens, width), BF16),
            pltpu.VMEM((chips * tokens, width), BF16),
            pltpu.VMEM((rows, width), BF16),
            pltpu.VMEM((rows, width), BF16),
            pltpu.SMEM((1,), jnp.int32),
            dma((4,)),
            dma((3 * count,)), dma((3 * count,)),
            dma((len(chunks) * count,)), dma((len(chunks) * count,)),
            dma((count,)), dma((count,)),
            dma((chips,)), dma((chips,)),
            dma((chips,)), dma((chips,)),
            dma((pieces,)), dma((pieces,)),
        ]
    results = pl.pallas_call(
        run,
        out_shape=(
            pltpu.VMEM((1, tokens, width), BF16),
            pltpu.VMEM((1, tokens, features), BF16),
            pltpu.VMEM((1, rows, width), F32),
        ),
        in_specs=[anywhere] * 4,
        out_specs=(in_vmem, in_vmem, in_vmem),
        scratch_shapes=scratch,
        compiler_params=pltpu.CompilerParams(
            collective_id=bit, has_side_effects=True, vmem_limit_bytes=40 * 2 ** 20),
        cost_estimate=pl.CostEstimate(
            flops=6 * every * rows * width, bytes_accessed=8 * 2 ** 20, transcendentals=0),
        name="step_bit_%d" % bit,
    )(step_index, activations, weights, cotangent)
    return pl.pallas_call(
        store_kernel,
        out_shape=tuple(jax.ShapeDtypeStruct(part.shape, part.dtype) for part in results),
        in_specs=[anywhere] * 3,
        out_specs=(anywhere, anywhere, anywhere),
        scratch_shapes=[dma((9,))],
        compiler_params=pltpu.CompilerParams(vmem_limit_bytes=2 ** 20),
        name="store",
    )(*results)


def body(count, activations, weights, cotangent, step_index):
    branches = [functools.partial(step_kernel, bit, count) for bit in range(BITS)]
    return lax.switch(step_index[0] % BITS, branches, activations, weights, cotangent, step_index)


def solution(mesh):
    split = P("rep", "fsdp", None)
    return jax.shard_map(
        functools.partial(body, mesh.shape["fsdp"]),
        mesh=mesh,
        in_specs=(split, split, split, P()),
        out_specs=(split, split, split),
        check_vma=False,
    )
```
